32 devices in a mesh: box: 8 (over y, x, core), dir: 4 (over z).
Axes of the slice: x: 2, y: 2, z: 4, core: 2. Of those that a mesh axis runs over, the one named last changes fastest.
Arguments:
- fine_out: float32 [1024, 2, 8192], P(('box', 'dir')), may hold values from -6 to 6
- theta_interp: float32 [128, 64], replicated, may hold values from -0.75 to 0.75
- phi_interp: float32 [128, 256], replicated, may hold values from -0.5 to 0.5
- shift_phase: float32 [8, 32768], P(None, 'dir'), may hold values from -3.140625 to 3.140625
- translation: float32 [316, 2, 32768], P(None, None, 'dir'), may hold values from -0.25 to 0.25
- upper_in: float32 [128, 2, 32768], P('box', None, 'dir'), may hold values from -6 to 6
- children: int32 [128, 8], P('box'), may hold values from 0 to 1023, as said below
- far_boxes: int32 [128, 28], P('box'), may hold values from 0 to 127, as said below
- far_offsets: int32 [128, 28], P('box'), may hold values from 0 to 315
Outputs:
- coarse_in: float32 [128, 2, 32768], P('box', None, 'dir')
- fine_in: float32 [1024, 2, 8192], P(('box', 'dir'))
The draws below stay inside these ranges and needn't reach their ends.
Inputs may be any that keep to these rules, and one draw needn't show every extreme that they name: Every fine box is named exactly once. The coarse boxes i * 16 to (i + 1) * 16 - 1 have as children exactly the fine boxes 8 * i * 16 to 8 * (i + 1) * 16 - 1. `far_boxes`: each row names 28 different coarse boxes, never the row's own box.
All inputs are finite; a program needn't handle non-finite values.
Results may differ from the reference program's by a relative error of at most 0.00008.
Values sent between devices are 32-bit elements; how exact they have to be, the bound alone decides.
A program may use at most 192 MiB of HBM per device.

```python
import jax
import jax.numpy as jnp
from jax import lax

TC = 128
PC = 256
TF = 64
PF = 128
NOFF = 316
LIST = 28
BOX_DEV = 16
KC = 32768
KF = 8192
BC = 128
BF = 1024


def draw_children(key, part):
    groups = BC // BOX_DEV
    span_rows = 8 * BOX_DEV
    scores = jax.random.randint(key, (groups, span_rows), 0, 1 << 20) * span_rows + jnp.arange(span_rows)[None, :]
    order = jnp.argsort(scores, axis=1)
    placed = order + (jnp.arange(groups) * span_rows)[:, None]
    return placed.reshape(BC, 8).astype(jnp.int32)


def draw_far_boxes(key, part):
    scores = jax.random.randint(key, (BC, BC - 1), 0, 1 << 20) * BC + jnp.arange(BC - 1)[None, :]
    order = jnp.argsort(scores, axis=1)[:, :LIST]
    own_box = jnp.arange(BC)[:, None]
    return (order + (order >= own_box).astype(order.dtype)).astype(jnp.int32)


def set_ends(array, stream_key, smallest, largest):
    longest = array.shape.index(max(array.shape))
    spots = []
    for shift in (0, 1):
        where = [jax.random.randint(jax.random.fold_in(stream_key, axis), (), 0, length) for axis, length in enumerate(array.shape)]
        where[longest] = (where[longest] + shift) % array.shape[longest]
        spots.append(tuple(where))
    return array.at[spots[0]].set(smallest).at[spots[1]].set(largest)


def levels(stream_key, dims, cuts, smallest, largest):
    factor_of = 1.0
    for position, blocks in cuts:
        heights = jax.random.uniform(jax.random.fold_in(jax.random.fold_in(stream_key, 6), position), (blocks,), jnp.float32, smallest / len(cuts), largest / len(cuts))
        factor_of = factor_of * jnp.repeat(jnp.exp(heights), dims[position] // blocks).reshape((-1,) + (1,) * (len(dims) - 1 - position))
    return factor_of


def normal_values(rng, dims, scale, limit, split=(), held_as=jnp.bfloat16):
    factor_of = levels(rng, dims, split, -0.22, 0.18) if split else 1.0
    array = jax.random.normal(rng, dims, jnp.float32) * scale * factor_of
    return jnp.minimum(jnp.maximum(array, -limit), limit).astype(held_as)


def setup_inputs(seed: int = 0) -> dict:
    key_list = jax.random.split(jax.random.key(seed), 10)
    return {
        "fine_out": normal_values(key_list[0], (BF, 2, KF), 1.0, 6.0, ((0, 32),), jnp.float32),
        "theta_interp": normal_values(key_list[1], (TC, TF), TF ** -0.5, 0.75, (), jnp.float32),
        "phi_interp": normal_values(key_list[2], (PF, PC), PF ** -0.5, 0.5, (), jnp.float32),
        "shift_phase": jnp.clip(jax.random.uniform(key_list[3], (8, KC), jnp.float32, -3.140625, 3.140625), -3.140625, 3.140625),
        "translation": normal_values(key_list[4], (NOFF, 2, KC), (16 * LIST) ** -0.5, 0.25, ((2, 4),), jnp.float32),
        "upper_in": normal_values(key_list[5], (BC, 2, KC), 1.0, 6.0, ((0, 8), (2, 4)), jnp.float32),
        "children": draw_children(jax.random.fold_in(key_list[9], 71), 0),
        "far_boxes": draw_far_boxes(jax.random.fold_in(key_list[9], 71), 0),
        "far_offsets": set_ends(jax.random.randint(key_list[8], (BC, LIST), 0, NOFF), jax.random.fold_in(key_list[8], 1), 0, NOFF - 1).astype(jnp.int32),
    }


HIGHEST_PREC = lax.Precision.HIGHEST


def interpolate(patterns, theta_map, phi_map):
    amount = patterns.shape[0]
    coarse_theta, fine_theta = theta_map.shape
    fine_phi, coarse_phi = phi_map.shape
    flat_rows = patterns.reshape(amount * 2 * fine_theta, fine_phi)
    along_phi = jnp.dot(flat_rows, phi_map, precision=HIGHEST_PREC, preferred_element_type=jnp.float32)
    along_phi = along_phi.reshape(amount, 2, fine_theta, coarse_phi)
    result = jnp.einsum("tu,ncus->ncts", theta_map, along_phi, precision=HIGHEST_PREC)
    return result.reshape(amount, 2, coarse_theta * coarse_phi)


def anterpolate(patterns, theta_map, phi_map):
    amount = patterns.shape[0]
    coarse_theta, fine_theta = theta_map.shape
    fine_phi, coarse_phi = phi_map.shape
    flat_rows = patterns.reshape(amount * 2 * coarse_theta, coarse_phi)
    along_phi = jnp.dot(flat_rows, phi_map.T, precision=HIGHEST_PREC, preferred_element_type=jnp.float32)
    along_phi = along_phi.reshape(amount, 2, coarse_theta, fine_phi)
    result = jnp.einsum("tu,ncts->ncus", theta_map, along_phi, precision=HIGHEST_PREC)
    return result.reshape(amount, 2, fine_theta * fine_phi)


def aggregate(child_rows, child_index, cosine, sine):
    picked = child_rows[child_index]
    real_part = jnp.sum(cosine * picked[:, :, 0] - sine * picked[:, :, 1], axis=1)
    imag_part = jnp.sum(sine * picked[:, :, 0] + cosine * picked[:, :, 1], axis=1)
    return jnp.stack([real_part, imag_part], axis=1)


def disaggregate(incoming, child_index, cosine, sine, total):
    real_in = incoming[:, None, 0]
    imag_in = incoming[:, None, 1]
    real_part = cosine * real_in + sine * imag_in
    imag_part = cosine * imag_in - sine * real_in
    width = incoming.shape[2]
    values = jnp.stack([real_part, imag_part], axis=2).reshape(-1, 2, width)
    empty = jnp.zeros((total, 2, width), jnp.float32)
    return empty.at[child_index.reshape(-1)].set(values)


def reference(fine_out, theta_interp, phi_interp, shift_phase, translation, upper_in, children, far_boxes, far_offsets):
    cosine = jnp.cos(shift_phase)
    sine = jnp.sin(shift_phase)
    child_rows = interpolate(fine_out, theta_interp, phi_interp)
    outgoing = aggregate(child_rows, children, cosine, sine)

    def translate_one(entry):
        far_index, far_kind = entry
        source_rows = outgoing[far_index]
        kernel_rows = translation[far_kind]
        real_part = jnp.sum(kernel_rows[:, 0] * source_rows[:, 0] - kernel_rows[:, 1] * source_rows[:, 1], axis=0)
        imag_part = jnp.sum(kernel_rows[:, 0] * source_rows[:, 1] + kernel_rows[:, 1] * source_rows[:, 0], axis=0)
        return jnp.stack([real_part, imag_part], axis=0)

    translated = lax.map(translate_one, (far_boxes, far_offsets))
    coarse_in = translated + upper_in
    child_in = disaggregate(coarse_in, children, cosine, sine, fine_out.shape[0])
    fine_in = anterpolate(child_in, theta_interp, phi_interp)
    return coarse_in, fine_in
```

```python
import functools

import jax
import jax.numpy as jnp
from jax import lax
from jax.experimental import pallas as pl
from jax.experimental.pallas import tpu as pltpu
from jax.sharding import PartitionSpec as P

F32, BF16, I32 = jnp.float32, jnp.bfloat16, jnp.int32
MESH = pl.DeviceIdType.MESH
VMEM_BYTES = 60 * 1024 * 1024
ROWS = 8
GROUP = 4
OCT = 8

COS = (
    0.999999999880854,
    -0.49999999845758136,
    0.04166666339221376,
    -0.001388886238622854,
    2.48005323812661e-05,
    -2.753445728365435e-07,
    2.0600835499376906e-09,
    -9.713911649043148e-12,
)
SIN = (
    0.9999999992304494,
    -0.166666659035747,
    0.008333320978968734,
    -0.00019840518737424315,
    2.7535517055355563e-06,
    -2.4725519533129986e-08,
    1.360099414116501e-10,
)


def split(x):
    hi = x.astype(BF16)
    return hi, (x - hi.astype(F32)).astype(BF16)


def dot3(a, b):
    (ah, al), (bh, bl) = a, b
    d = functools.partial(jnp.dot, preferred_element_type=F32)
    return d(ah, bh) + (d(ah, bl) + d(al, bh))


def horner(y, coefficients):
    r = jnp.full_like(y, coefficients[-1])
    for c in coefficients[-2::-1]:
        r = r * y + c
    return r


def rows_view(x):
    n, _, k = x.shape
    return x.reshape(n, 2, k // 128, 128).transpose(0, 2, 1, 3).reshape(n, k // 64, 128)


def rows_unview(x):
    n, r, _ = x.shape
    return x.reshape(n, r // 2, 2, 128).transpose(0, 2, 1, 3).reshape(n, 2, r * 64)


def neighbours(v):
    return pltpu.roll(v, 7, v.ndim - 2), pltpu.roll(v, 1, v.ndim - 2)


def even_rows(shape):
    return lax.broadcasted_iota(I32, shape, len(shape) - 2) % 2 == 0


def kernel(
    dims,
    itab,
    ftab,
    far_ref,
    phase_ref,
    x_ref,
    phi_ref,
    theta_ref,
    thetat_ref,
    phit_ref,
    upper_ref,
    trans_ref,
    coarse_ref,
    fine_ref,
    trans,
    farr,
    fars,
    zp,
    pf,
    cc,
    cs,
    alh,
    all_,
    th,
    tl_,
    tth,
    ttl,
    wide,
    widet,
    mask,
    maskt,
    sb,
    part,
    ar,
    qa,
    ql,
    qs,
    ts,
    ta,
    cg,
    xl,
    kl,
    fa,
    sem_tr,
    sem_fs,
    far_s,
    far_r,
    zp_s,
    zp_r,
    pf_s,
    pf_r,
    up_s,
    up_r,
    q_s,
    q_r,
    t_s,
    t_r,
    dr_s,
    dl_s,
    d_r,
):
    nb, nd, C, n, parents, many, bits = dims
    R = nd * GROUP * 8
    b, z = lax.axis_index("box"), lax.axis_index("dir")
    g, h = b % GROUP, b // GROUP
    pr = OCT * 16 // nb
    PERM, OCTS, PARENT, OCTANT, LAST = (i * n for i in range(5))

    def remote(src, dst, ss, rs, dev):
        return pltpu.make_async_remote_copy(
            src_ref=src, dst_ref=dst, send_sem=ss, recv_sem=rs, device_id=dev, device_id_type=MESH
        )

    def zp_copy(c, j):
        to = (z + j) % nd
        return remote(
            phase_ref.at[c, pl.ds(pl.multiple_of(b * pr, 8), pr)],
            zp.at[c, z],
            zp_s.at[c, j],
            zp_r.at[c, j],
            (b, to),
        )

    def pf_copy(c, j):
        return remote(zp.at[c], pf.at[c, b], pf_s.at[c, j], pf_r.at[c, j], (b ^ j, z))

    def far_copy(j):
        return remote(far_ref, farr.at[g], far_s.at[j], far_r.at[j], (b ^ j, z))

    def right_copy(c, d):
        return remote(part.at[c, d], ar.at[c, d], up_s.at[c, d], up_r.at[c, d], (b, z + 1))

    def left_copy(c, d):
        slot = jnp.where(z - 1 == d, nd, d)
        return remote(part.at[c, d], ar.at[c, slot], up_s.at[c, d], up_r.at[c, slot], (b, z - 1))

    def up_wait(c, slot):
        return remote(part.at[c, 0], ar.at[c, slot], up_s.at[c, 0], up_r.at[c, slot], (b, z))

    def q_copy(c, j):
        to = b ^ j
        return remote(
            part.at[c, z, to % GROUP], qa.at[c, b], q_s.at[c, j], q_r.at[c, j], (to, z)
        )

    def t_copy(c, j):
        return remote(ts.at[c, g ^ j], ta.at[c, g], t_s.at[c, j], t_r.at[c, j], (b ^ j, z))

    def down_right(c, d):
        return remote(cg.at[c, d], cg.at[c, d], dr_s.at[c, d], d_r.at[c, d], (b, z + 1))

    def down_left(c, d):
        return remote(cg.at[c, d], cg.at[c, d], dl_s.at[c, d], d_r.at[c, d], (b, z - 1))

    def trans_copy(c):
        row = pl.multiple_of((c * GROUP + g) * 8, 8)
        return pltpu.make_async_copy(trans_ref.at[:, pl.ds(row, 8)], trans.at[c], sem_tr.at[c])

    for c in range(C):
        trans_copy(c).start()

    barrier = pltpu.get_barrier_semaphore()
    for j in range(1, nb):
        pl.semaphore_signal(barrier, inc=1, device_id=(b ^ j, z), device_id_type=MESH)
    for j in range(1, nd):
        pl.semaphore_signal(barrier, inc=1, device_id=(b, (z + j) % nd), device_id_type=MESH)
    pl.semaphore_wait(barrier, nb + nd - 2)

    for c in range(C):
        for j in range(1, nd):
            zp_copy(c, j).start()
    for j in range(1, GROUP):
        far_copy(j).start()
    for c in range(C):
        zp[c, z] = phase_ref[c, pl.ds(pl.multiple_of(b * pr, 8), pr), :]
    farr[g] = far_ref[...]

    phi = split(phi_ref[...])
    many_children = 4

    def along(i, _):
        rows = x_ref.shape[1]
        v = x_ref[pl.ds(i * many_children, many_children)].reshape(many_children * rows, 128)
        y = dot3(split(v), phi)
        for q in range(many_children):
            for half in range(2):
                hi, lo = split(y[q * rows : (q + 1) * rows, half * 128 : (half + 1) * 128])
                alh[i * many_children + q, half * rows : (half + 1) * rows, :] = hi
                all_[i * many_children + q, half * rows : (half + 1) * rows, :] = lo
        return 0

    def phases_on(c):
        for j in range(1, nd):
            zp_copy(c, j).wait_recv()
        for j in range(1, nb):
            pf_copy(c, j).start()
        pf[c, b] = zp[c]

    def shifts(c):
        for j in range(1, nb):
            pf_copy(c, j).wait_recv()
        per = 16 // pr

        def body(o, _):
            for d in range(nd):
                for j in range(per):
                    v = pf[c, o * per + j, d]
                    y = v * v
                    co, si = horner(y, COS), v * horner(y, SIN)
                    for p in range(2):
                        where = pl.ds(d * 32 + 2 * j * pr + p, pr, stride=2)
                        cc[c, o, where, :] = co
                        cs[c, o, where, :] = si
            return 0

        lax.fori_loop(0, OCT, body, 0)

    tc, tf = theta_ref.shape
    tl = tc // nd

    def axis(shape, d):
        return lax.broadcasted_iota(I32, shape, d)

    def ones(shape, hit):
        return jnp.where(hit, 1.0, 0.0).astype(BF16)

    def fine_row(i):
        return (i >> 1) & (tf - 1)

    def polar_row(c, r):
        r = r & (R - 1)
        return (r >> 5) * tl + c * ROWS + ((r >> 2) & (ROWS - 1))

    def masks():
        shape = (2 * R, 4 * tf)
        r, k = axis(shape, 0), axis(shape, 1)
        p, plane, turned = r & 1, k & 1, r >= R
        same_half = ((r >> 1) & 1) == jnp.where(k >= 2 * tf, 1, 0)
        sign = jnp.where(turned & (p == 0), -1.0, 1.0)
        hit = same_half & ((p != plane) == turned)
        mask[...] = jnp.where(hit, sign, 0.0).astype(BF16)
        shape = (4 * tf, R)
        k, r = axis(shape, 0), axis(shape, 1)
        hit = (((r >> 1) & 1) == jnp.where(k >= 2 * tf, 1, 0)) & ((r & 1) == (k & 1))
        maskt[...] = ones(shape, hit)
        shape = (tf, 4 * tf)
        w = ones(shape, fine_row(axis(shape, 1)) == axis(shape, 0))
        shape = (4 * tf, tf)
        wt = ones(shape, fine_row(axis(shape, 0)) == axis(shape, 1))
        for v, out in zip(split(theta_ref[...]), (0, 1)):
            wide[out] = d32(v, w).astype(BF16)
        for v, out in zip(split(thetat_ref[...]), (0, 1)):
            widet[out] = d32(wt, v).astype(BF16)

    d32 = functools.partial(jnp.dot, preferred_element_type=F32)

    def spread_map(c):
        shape = (2 * R, tc)
        pick = ones(shape, polar_row(c, axis(shape, 0)) == axis(shape, 1))
        for i, out in enumerate((th, tl_)):
            out[...] = d32(pick, wide[i]).astype(BF16) * mask[...]

    def spread_map_back(c):
        shape = (tc, R)
        pick = ones(shape, polar_row(c, axis(shape, 1)) == axis(shape, 0))
        for i, out in enumerate((tth, ttl)):
            out[...] = d32(widet[i], pick).astype(BF16) * maskt[...]

    def aggregate(c):
        spread_map(c)

        def body(kk, acc):
            k = 2 * kk
            i0, i1 = itab[PERM + k], itab[PERM + k + 1]
            rh = jnp.concatenate([alh[i0], alh[i1]], axis=1)
            rl = jnp.concatenate([all_[i0], all_[i1]], axis=1)
            v = dot3((th[...], tl_[...]), (rh, rl))
            for q in range(2):
                o = itab[OCTS + k + q]
                lanes = slice(q * 128, (q + 1) * 128)
                y = cc[c, o] * v[:R, lanes] + cs[c, o] * v[R:, lanes]
                acc = acc * ftab[k + q] + y
                sb[k + q] = acc
            return acc

        lax.fori_loop(0, n // 2, body, jnp.zeros((R, 128), F32))

        def pick(p, _):
            v = sb[itab[LAST + p]] * ftab[n + p]
            part[c, :, :, p] = v.reshape(nd, GROUP, 8, 128)
            return 0

        lax.fori_loop(0, parents, pick, 0)

    def add(c, d, slot):
        def body(k, _):
            part[c, d, k] = part[c, d, k] + ar[c, slot, k]
            return 0

        lax.fori_loop(0, GROUP, body, 0)

    def send_ends(c):
        @pl.when(z == 0)
        def _():
            for d in range(nd - 1, 0, -1):
                right_copy(c, d).start()

        @pl.when(z == nd - 1)
        def _():
            for d in range(nd - 1):
                left_copy(c, d).start()

    def hop(c, k):
        d = nd - 1 - k

        @pl.when(jnp.logical_and(z < d, z > 0))
        def _():
            up_wait(c, d).wait_recv()
            add(c, d, d)
            right_copy(c, d).start()

        @pl.when(jnp.logical_and(z > k, z < nd - 1))
        def _():
            up_wait(c, k).wait_recv()
            add(c, k, k)
            left_copy(c, k).start()

    def finish_up(c):
        @pl.when(z > 0)
        def _():
            up_wait(c, z).wait_recv()
            add(c, z, z)

        @pl.when(z < nd - 1)
        def _():
            up_wait(c, nd).wait_recv()
            add(c, z, nd)

        for j in range(1, nb):
            q_copy(c, j).start()
        qa[c, b] = part[c, z, g]

    def translate(c):
        if c == 0:
            for j in range(1, GROUP):
                far_copy(j).wait_recv()
            move = pltpu.make_async_copy(farr, fars, sem_fs)
            move.start()
            move.wait()
            for i in range(C):
                trans_copy(i).wait()
        for j in range(1, nb):
            q_copy(c, j).wait_recv()

        def stage(s, _):
            v = qa[c, s]
            below, above = neighbours(v)
            ql[pl.ds(s * parents, parents)] = v
            qs[pl.ds(s * parents, parents)] = jnp.where(even_rows(v.shape), below, above)
            return 0

        lax.fori_loop(0, nb, stage, 0)
        even = even_rows((8, 128))
        for jg in range(GROUP):

            def body(p, _):
                u = w = None
                for l in range(many):
                    code = fars[jg, p, l]
                    f, kind = code & ((1 << bits) - 1), code >> bits
                    a = trans[c, kind]
                    r, i = a * ql[f], a * qs[f]
                    u = r if u is None else u + r
                    w = i if w is None else w + i
                re = u - pltpu.roll(u, 7, 0)
                im = w + pltpu.roll(w, 1, 0)
                ts[c, jg, p] = jnp.where(even, re, im)
                return 0

            lax.fori_loop(0, parents, body, 0)
        for j in range(1, GROUP):
            t_copy(c, j).start()
        ta[c, g] = ts[c, g]

    def coarse(c):
        for j in range(1, GROUP):
            t_copy(c, j).wait_recv()

        def body(p, _):
            rows = pl.ds(c * GROUP * 8, GROUP * 8)
            v = ta[c, :, p] + upper_ref[p, rows, :].reshape(GROUP, 8, 128)
            coarse_ref[p, rows, :] = v.reshape(GROUP * 8, 128)
            cg[c, z, :, p] = v
            return 0

        lax.fori_loop(0, parents, body, 0)

        @pl.when(z < nd - 1)
        def _():
            down_right(c, z).start()

        @pl.when(z > 0)
        def _():
            down_left(c, z).start()

    def pass_down(c, k):
        @pl.when(z >= k)
        def _():
            down_right(c, z - k).wait_recv()

            @pl.when(z < nd - 1)
            def _():
                down_right(c, z - k).start()

        @pl.when(z + k < nd)
        def _():
            down_left(c, z + k).wait_recv()

            @pl.when(z > 0)
            def _():
                down_left(c, z + k).start()

    def disaggregate(c):
        spread_map_back(c)

        def stage(p, _):
            v = cg[c, :, :, p].reshape(nd * GROUP, 8, 128)
            below, above = neighbours(v)
            xl[p] = v.reshape(R, 128)
            kl[p] = jnp.where(even_rows(v.shape), below, -above).reshape(R, 128)
            return 0

        lax.fori_loop(0, parents, stage, 0)
        phit = split(phit_ref[...]) if c == C - 1 else None

        def body(ii, _):
            ys = []
            for q in range(2):
                p, o = itab[PARENT + 2 * ii + q], itab[OCTANT + 2 * ii + q]
                ys.append(cc[c, o] * xl[p] + cs[c, o] * kl[p])
            v = dot3((tth[...], ttl[...]), split(jnp.concatenate(ys, axis=1)))
            for q in range(2):
                w = v[:, q * 128 : (q + 1) * 128]
                if c > 0:
                    w = w + fa[2 * ii + q]
                if c < C - 1:
                    fa[2 * ii + q] = w
                else:
                    half = w.shape[0] // 2
                    line = jnp.concatenate([w[:half], w[half:]], axis=1)
                    fine_ref[2 * ii + q] = dot3(split(line), phit)
            return 0

        lax.fori_loop(0, n // 2, body, 0)

    masks()
    lax.fori_loop(0, n // many_children, along, 0)
    for c in range(C):
        phases_on(c)
    shifts(0)
    aggregate(0)
    send_ends(0)
    for s in range(C):
        if s + 1 < C:
            shifts(s + 1)
            aggregate(s + 1)
            send_ends(s + 1)
        if s >= 1:
            translate(s - 1)
        if s >= 2:
            for k in range(2, nd):
                pass_down(s - 2, k)
        hop(s, 0)
        if s >= 1:
            coarse(s - 1)
        for k in range(1, nd - 1):
            hop(s, k)
        if s >= 2:
            disaggregate(s - 2)
        finish_up(s)
        if s >= 1:
            pass_down(s - 1, 1)
    translate(C - 1)
    coarse(C - 1)
    if C >= 2:
        for k in range(2, nd):
            pass_down(C - 2, k)
        disaggregate(C - 2)
    for k in range(1, nd):
        pass_down(C - 1, k)
    disaggregate(C - 1)

    for j in range(1, GROUP):
        far_copy(j).wait_send()

    def drain(c, _):
        for j in range(1, nd):
            zp_copy(c, j).wait_send()
        for j in range(1, nb):
            pf_copy(c, j).wait_send()
            q_copy(c, j).wait_send()
        for j in range(1, GROUP):
            t_copy(c, j).wait_send()
        for d in range(nd):

            @pl.when(d > z)
            def _():
                right_copy(c, d).wait_send()

            @pl.when(d < z)
            def _():
                left_copy(c, d).wait_send()

            @pl.when(jnp.logical_and(d <= z, z < nd - 1))
            def _():
                down_right(c, d).wait_send()

            @pl.when(jnp.logical_and(d >= z, z > 0))
            def _():
                down_left(c, d).wait_send()

        return 0

    lax.fori_loop(0, C, drain, 0)


def shards(
    fine_out,
    theta_interp,
    phi_interp,
    shift_phase,
    translation,
    upper_in,
    children,
    far_boxes,
    far_offsets,
):
    n = fine_out.shape[0]
    tc, tf = theta_interp.shape
    pf_, pc = phi_interp.shape
    parents, many = far_boxes.shape
    nb, nd = lax.axis_size("box"), lax.axis_size("dir")
    noff = translation.shape[0]
    tl = tc // nd
    C = tl // ROWS
    R = nd * GROUP * 8
    bits = (nb * parents - 1).bit_length()

    flat = (children % (n * nd)).reshape(-1)
    own = lax.axis_index("dir") * n + jnp.arange(n, dtype=I32)
    slots = jnp.arange(flat.shape[0], dtype=I32)
    ids = jnp.arange(n, dtype=I32)
    slot = jnp.sum(jnp.where(flat[None, :] == own[:, None], slots[None, :], 0), axis=1)
    before = slot[None, :] < slot[:, None]
    rank = jnp.sum(before.astype(I32), axis=1)
    parent, octant = slot // OCT, slot % OCT
    same = jnp.any(before & (parent[None, :] == parent[:, None]), axis=1).astype(I32)
    at = rank[None, :] == ids[:, None]
    packed = jnp.sum(jnp.where(at, (ids * OCT + octant)[None, :] * 2 + same[None, :], 0), axis=1)
    boxes = jnp.arange(parents, dtype=I32)
    upto = jnp.sum((parent[None, :] <= boxes[:, None]).astype(I32), axis=1)
    has = jnp.any(parent[None, :] == boxes[:, None], axis=1)
    itab = jnp.concatenate(
        [packed // (2 * OCT), packed // 2 % OCT, parent, octant, jnp.maximum(upto - 1, 0)]
    )
    ftab = jnp.concatenate([(packed % 2).astype(F32), has.astype(F32)])
    far = jnp.pad(far_boxes + (far_offsets << bits), ((0, 0), (0, 128 - many)))

    phases = (
        shift_phase.reshape(OCT, C, ROWS * 2, 128).transpose(1, 0, 2, 3).reshape(C, OCT * 16, 128)
    )

    vmem, smem, hbm = (
        pl.BlockSpec(memory_space=m) for m in (pltpu.VMEM, pltpu.SMEM, pl.ANY)
    )
    dma = pltpu.SemaphoreType.DMA
    tile = (GROUP, parents, 8, 128)
    rows, fine_rows = C * GROUP * 8, tf * 2
    coarse_in, fine_in = pl.pallas_call(
        functools.partial(kernel, (nb, nd, C, n, parents, many, bits)),
        in_specs=[smem, smem] + [vmem] * 8 + [hbm],
        out_specs=[vmem, vmem],
        out_shape=[
            jax.ShapeDtypeStruct((parents, rows, 128), F32),
            jax.ShapeDtypeStruct((n, fine_rows, pf_), F32),
        ],
        scratch_shapes=[
            pltpu.VMEM((C, noff, 8, 128), F32),
            pltpu.VMEM((GROUP, parents, 128), I32),
            pltpu.SMEM((GROUP, parents, 128), I32),
            pltpu.VMEM((C, nd, OCT * 16 // nb, 128), F32),
            pltpu.VMEM((C, nb, nd, OCT * 16 // nb, 128), F32),
            pltpu.VMEM((C, OCT, R, 128), F32),
            pltpu.VMEM((C, OCT, R, 128), F32),
            pltpu.VMEM((n, 2 * fine_rows, 128), BF16),
            pltpu.VMEM((n, 2 * fine_rows, 128), BF16),
            pltpu.VMEM((2 * R, 4 * tf), BF16),
            pltpu.VMEM((2 * R, 4 * tf), BF16),
            pltpu.VMEM((4 * tf, R), BF16),
            pltpu.VMEM((4 * tf, R), BF16),
            pltpu.VMEM((2, tc, 4 * tf), BF16),
            pltpu.VMEM((2, 4 * tf, tc), BF16),
            pltpu.VMEM((2 * R, 4 * tf), BF16),
            pltpu.VMEM((4 * tf, R), BF16),
            pltpu.VMEM((n, R, 128), F32),
            pltpu.VMEM((C, nd) + tile, F32),
            pltpu.VMEM((C, nd + 1) + tile, F32),
            pltpu.VMEM((C, nb) + tile[1:], F32),
            pltpu.VMEM((nb * parents, 8, 128), F32),
            pltpu.VMEM((nb * parents, 8, 128), F32),
            pltpu.VMEM((C,) + tile, F32),
            pltpu.VMEM((C,) + tile, F32),
            pltpu.VMEM((C, nd) + tile, F32),
            pltpu.VMEM((parents, R, 128), F32),
            pltpu.VMEM((parents, R, 128), F32),
            pltpu.VMEM((n, 4 * tf, 128), F32),
            dma((C,)),
            dma,
            dma((GROUP,)),
            dma((GROUP,)),
            dma((C, nd)),
            dma((C, nd)),
            dma((C, nb)),
            dma((C, nb)),
            dma((C, nd)),
            dma((C, nd + 1)),
            dma((C, nb)),
            dma((C, nb)),
            dma((C, GROUP)),
            dma((C, GROUP)),
            dma((C, nd)),
            dma((C, nd)),
            dma((C, nd)),
        ],
        compiler_params=pltpu.CompilerParams(
            collective_id=0, has_side_effects=True, vmem_limit_bytes=VMEM_BYTES
        ),
    )(
        itab,
        ftab,
        far,
        phases,
        rows_view(fine_out),
        phi_interp,
        theta_interp,
        theta_interp.T,
        phi_interp.T,
        rows_view(upper_in),
        rows_view(translation),
    )
    return rows_unview(coarse_in), rows_unview(fine_in)


def solution(mesh):
    placed = (
        P(("box", "dir"), None, None),
        P(),
        P(),
        P(None, "dir"),
        P(None, None, "dir"),
        P("box", None, "dir"),
        P("box", None),
        P("box", None),
        P("box", None),
    )
    return jax.shard_map(
        shards,
        mesh=mesh,
        in_specs=placed,
        out_specs=(P("box", None, "dir"), P(("box", "dir"), None, None)),
        check_vma=False,
    )
```

```python
import functools

import jax
import jax.numpy as jnp
from jax import lax
from jax.experimental import pallas as pl
from jax.experimental.pallas import tpu as pltpu
from jax.sharding import PartitionSpec as P

F32, BF16, I32 = jnp.float32, jnp.bfloat16, jnp.int32
MESH = pl.DeviceIdType.MESH
VMEM_BYTES = 60 * 1024 * 1024
FINE = 2
ORDERS = {
    (4, 8): (0, 0, 0, 0, 1, 0, 3, 1, 1, 0, 3, 1, 3, 5, 1, 2, 1, 2, 3, 2, 0, 2, 3, 1, 0, 2, 3, 1, 2, 5, 3, 0, 1, 5, 2, 4, 0, 5, 5, 2, 4, 0, 4, 1, 7, 4, 2, 3, 4, 5, 0, 3, 6, 4, 5, 6, 1, 7, 6, 3, 4, 6, 7, 6, 7, 5, 3, 2, 7, 1, 6, 3, 2, 4, 6, 7, 2, 5, 7, 4, 6, 5, 6, 7, 5, 4, 6, 7, 5, 6, 4, 7, 6, 4, 7, 7),
    (4, 4): (2, 2, 0, 0, 2, 0, 1, 2, 0, 1, 0, 2, 0, 2, 3, 0, 1, 3, 1, 1, 2, 0, 3, 1, 3, 2, 3, 0, 2, 1, 3, 1, 0, 1, 3, 2, 0, 3, 1, 2, 3, 1, 0, 2, 3, 1, 3, 3),
}
OCT = 8

COS = (
    0.999999999880854,
    -0.49999999845758136,
    0.04166666339221376,
    -0.001388886238622854,
    2.48005323812661e-05,
    -2.753445728365435e-07,
    2.0600835499376906e-09,
    -9.713911649043148e-12,
)
SIN = (
    0.9999999992304494,
    -0.166666659035747,
    0.008333320978968734,
    -0.00019840518737424315,
    2.7535517055355563e-06,
    -2.4725519533129986e-08,
    1.360099414116501e-10,
)


def split(x):
    hi = x.astype(BF16)
    return hi, (x - hi.astype(F32)).astype(BF16)


def dot3(a, b, turned=False):
    (ah, al), (bh, bl) = a, b
    sums = (((1,), (1 if turned else 0,)), ((), ()))
    d = functools.partial(lax.dot_general, dimension_numbers=sums, preferred_element_type=F32)
    return d(ah, bh) + (d(ah, bl) + d(al, bh))


def horner(y, coefficients):
    r = jnp.full_like(y, coefficients[-1])
    for c in coefficients[-2::-1]:
        r = r * y + c
    return r


def pair_of(rows, chunks):
    return 2 if rows <= 64 and chunks % 2 == 0 else 1


def rows_view(x):
    n, _, k = x.shape
    return x.reshape(n, 2, k // 128, 128).transpose(0, 2, 1, 3).reshape(n, k // 64, 128)


def rows_unview(x):
    n, r, _ = x.shape
    return x.reshape(n, r // 2, 2, 128).transpose(0, 2, 1, 3).reshape(n, 2, r * 64)


def neighbours(v):
    return pltpu.roll(v, 7, v.ndim - 2), pltpu.roll(v, 1, v.ndim - 2)


def even_rows(shape):
    return lax.broadcasted_iota(I32, shape, len(shape) - 2) % 2 == 0


def kernel(
    dims,
    children_ref,
    boxes_ref,
    kinds_ref,
    phase_ref,
    x_ref,
    phi_ref,
    thetat_ref,
    upper_ref,
    trans_ref,
    coarse_ref,
    fine_ref,
    trans,
    tabv,
    itab,
    farr,
    fars,
    zp,
    pf,
    cc,
    cs,
    alh,
    all_,
    th,
    tl_,
    tth,
    wide,
    widet,
    mask,
    maskt,
    sb,
    part,
    ar,
    qa,
    ql,
    ts,
    ta,
    cg,
    xl,
    kl,
    fa,
    sem_tr,
    sem_fs,
    sem_tab,
    far_s,
    far_r,
    zp_s,
    zp_r,
    pf_s,
    pf_r,
    up_s,
    up_r,
    q_s,
    q_r,
    t_s,
    t_r,
    dr_s,
    dl_s,
    d_r,
):
    nb, nd, C, ROWS, n, parents, many, bits = dims
    GROUP = ROWS // 2
    PER = GROUP * 8
    R = nd * PER
    PAIR = pair_of(R, C)
    b, z = lax.axis_index("box"), lax.axis_index("dir")
    g, h = b % GROUP, b // GROUP
    pr = OCT * 2 * ROWS // nb
    PERM, OCTS, PARENT, OCTANT, LAST, KEEP, HAS = range(7)

    def remote(src, dst, ss, rs, dev):
        return pltpu.make_async_remote_copy(
            src_ref=src, dst_ref=dst, send_sem=ss, recv_sem=rs, device_id=dev, device_id_type=MESH
        )

    def zp_copy(c, j):
        to = (z + j) % nd
        return remote(
            phase_ref.at[c, pl.ds(pl.multiple_of(b * pr, 8), pr)],
            zp.at[c, z],
            zp_s.at[c, j],
            zp_r.at[c, j],
            (b, to),
        )

    def pf_copy(c, j):
        return remote(zp.at[c], pf.at[c, b], pf_s.at[c, j], pf_r.at[c, j], (b ^ j, z))

    def far_copy(j):
        return remote(farr.at[g], farr.at[g], far_s.at[j], far_r.at[j], (b ^ j, z))

    def right_copy(c, d):
        return remote(part.at[c, d], ar.at[c, d], up_s.at[c, d], up_r.at[c, d], (b, z + 1))

    def left_copy(c, d):
        slot = jnp.where(z - 1 == d, nd, d)
        return remote(part.at[c, d], ar.at[c, slot], up_s.at[c, d], up_r.at[c, slot], (b, z - 1))

    def up_wait(c, slot):
        return remote(part.at[c, 0], ar.at[c, slot], up_s.at[c, 0], up_r.at[c, slot], (b, z))

    def q_copy(c, j):
        to = b ^ j
        return remote(
            part.at[c, z, to % GROUP], qa.at[c, b], q_s.at[c, j], q_r.at[c, j], (to, z)
        )

    def t_copy(c, j):
        return remote(ts.at[c, g ^ j], ta.at[c, g], t_s.at[c, j], t_r.at[c, j], (b ^ j, z))

    def down_right(c, d):
        return remote(cg.at[c, d], cg.at[c, d], dr_s.at[c, d], d_r.at[c, d], (b, z + 1))

    def down_left(c, d):
        return remote(cg.at[c, d], cg.at[c, d], dl_s.at[c, d], d_r.at[c, d], (b, z - 1))

    def trans_copy(c):
        row = pl.multiple_of((c * GROUP + g) * 8, 8)
        return pltpu.make_async_copy(trans_ref.at[:, pl.ds(row, 8)], trans.at[c], sem_tr.at[c])

    for c in range(C):
        trans_copy(c).start()

    farr[g, :, 0:many] = boxes_ref[...] + (kinds_ref[...] << bits)
    barrier = pltpu.get_barrier_semaphore()
    for j in range(1, nb):
        pl.semaphore_signal(barrier, inc=1, device_id=(b ^ j, z), device_id_type=MESH)
    for j in range(1, nd):
        pl.semaphore_signal(barrier, inc=1, device_id=(b, (z + j) % nd), device_id_type=MESH)
    pl.semaphore_wait(barrier, nb + nd - 2)

    for c in range(C):
        for j in range(1, nd):
            zp_copy(c, j).start()
    for j in range(1, GROUP):
        far_copy(j).start()
    for c in range(C):
        zp[c, z] = phase_ref[c, pl.ds(pl.multiple_of(b * pr, 8), pr), :]

    lanes = lax.broadcasted_iota(I32, (1, 128), 1)

    def table(p, carry):
        k, rows = carry[0], list(carry[1:])
        first = k
        for o in range(OCT):
            local = lax.rem(children_ref[o, p], n * nd) - z * n
            own = jnp.logical_and(local >= 0, local < n)
            here, at = lanes == jnp.where(own, k, -1), lanes == jnp.where(own, local, -1)
            rows[PERM] = jnp.where(here, local, rows[PERM])
            rows[OCTS] = jnp.where(here, o, rows[OCTS])
            rows[KEEP] = jnp.where(here, jnp.where(k > first, 1, 0), rows[KEEP])
            rows[PARENT] = jnp.where(at, p, rows[PARENT])
            rows[OCTANT] = jnp.where(at, o, rows[OCTANT])
            k = k + jnp.where(own, 1, 0)
        rows[LAST] = jnp.where(lanes == p, jnp.clip(k - 1, 0, n - 1), rows[LAST])
        rows[HAS] = jnp.where(lanes == p, jnp.where(k > first, 1, 0), rows[HAS])
        return (k, *rows)

    none = jnp.zeros((1, 128), I32)
    found = lax.fori_loop(0, parents, table, (jnp.int32(0), *[none] * 7))
    for i in range(7):
        tabv[i : i + 1, :] = found[1 + i]
    tabv[7:8, :] = none
    to_scalars = pltpu.make_async_copy(tabv, itab, sem_tab)
    to_scalars.start()

    phi = split(phi_ref[...])
    many_children = 4

    def along(i, _):
        rows = x_ref.shape[1]
        v = x_ref[pl.ds(i * many_children, many_children)].reshape(many_children * rows, 128)
        y = dot3(split(v), phi)
        for q in range(many_children):
            for half in range(2):
                hi, lo = split(y[q * rows : (q + 1) * rows, half * 128 : (half + 1) * 128])
                alh[i * many_children + q, half * rows : (half + 1) * rows, :] = hi
                all_[i * many_children + q, half * rows : (half + 1) * rows, :] = lo
        return 0

    def phases_on(c):
        for j in range(1, nd):
            zp_copy(c, j).wait_recv()
        for j in range(1, nb):
            pf_copy(c, j).start()
        pf[c, b] = zp[c]

    def shifts(c):
        for j in range(1, nb):
            pf_copy(c, j).wait_recv()
        per = 2 * ROWS // pr

        def body(o, _):
            for d in range(nd):
                for j in range(per):
                    v = pf[c, o * per + j, d]
                    y = v * v
                    co, si = horner(y, COS), v * horner(y, SIN)
                    for p in range(2):
                        where = pl.ds(d * PER + 2 * j * pr + p, pr, stride=2)
                        cc[c, o, where, :] = co
                        cs[c, o, where, :] = si
            return 0

        lax.fori_loop(0, OCT, body, 0)

    tf, tc = thetat_ref.shape
    tl = tc // nd

    def axis(shape, d):
        return lax.broadcasted_iota(I32, shape, d)

    def ones(shape, hit):
        return jnp.where(hit, 1.0, 0.0).astype(BF16)

    def fine_row(i):
        return (i >> 1) & (tf - 1)

    def polar_row(c, r):
        c, r = c + (r >> (R.bit_length() - 1)), r & (R - 1)
        return (r >> (PER.bit_length() - 1)) * tl + c * ROWS + ((r >> 2) & (ROWS - 1))

    def masks():
        shape = (PAIR * R, 4 * tf)
        r, k = axis(shape, 0), axis(shape, 1)
        hit = (((r >> 1) & 1) == jnp.where(k >= 2 * tf, 1, 0)) & ((r & 1) == (k & 1))
        mask[...] = ones(shape, hit)
        shape = (4 * tf, R)
        k, r = axis(shape, 0), axis(shape, 1)
        hit = (((r >> 1) & 1) == jnp.where(k >= 2 * tf, 1, 0)) & ((r & 1) == (k & 1))
        maskt[...] = ones(shape, hit)
        shape = (tf, 4 * tf)
        w = ones(shape, fine_row(axis(shape, 1)) == axis(shape, 0))
        shape = (4 * tf, tf)
        wt = ones(shape, fine_row(axis(shape, 0)) == axis(shape, 1))
        for v, out in zip(split(thetat_ref[...].T), (0, 1)):
            wide[out] = d32(v, w).astype(BF16)
        for v, out in zip(split(thetat_ref[...]), (0, 1)):
            widet[out] = d32(wt, v).astype(BF16)

    d32 = functools.partial(jnp.dot, preferred_element_type=F32)

    def spread_map(c):
        shape = (PAIR * R, tc)
        pick = ones(shape, polar_row(c, axis(shape, 0)) == axis(shape, 1))
        for i, out in enumerate((th, tl_)):
            out[...] = d32(pick, wide[i]).astype(BF16) * mask[...]

    def spread_map_back(c):
        shape = (tc, R)
        pick = ones(shape, polar_row(c, axis(shape, 1)) == axis(shape, 0))
        for i, source in enumerate((0, 0, 1)):
            tth[:, i * R : (i + 1) * R] = d32(widet[source], pick).astype(BF16) * maskt[...]

    gathered = set()

    def aggregate(c):
        c = c // PAIR * PAIR
        if c in gathered:
            return
        gathered.add(c)
        for e in range(PAIR):
            shifts(c + e)
        spread_map(c)

        def body(kk, sums):
            k = 2 * kk
            i0, i1 = itab[PERM, k], itab[PERM, k + 1]
            rh = jnp.concatenate([alh[i0], alh[i1]], axis=1)
            rl = jnp.concatenate([all_[i0], all_[i1]], axis=1)
            v = dot3((th[...], tl_[...]), (rh, rl))
            for q in range(2):
                o, keep = itab[OCTS, k + q], itab[KEEP, k + q].astype(F32)
                for e in range(PAIR):
                    w = v[e * R : (e + 1) * R, q * 128 : (q + 1) * 128]
                    sums[2 * e] = sums[2 * e] * keep + cc[c + e, o] * w
                    sums[2 * e + 1] = sums[2 * e + 1] * keep + cs[c + e, o] * w
                for e in range(2 * PAIR):
                    sb[k + q, e] = sums[e]
            return sums

        lax.fori_loop(0, n // 2, body, [jnp.zeros((R, 128), F32)] * (2 * PAIR))

        def pick(p, _):
            last, has = itab[LAST, p], itab[HAS, p].astype(F32)
            for e in range(PAIR):
                v, w = (sb[last, 2 * e + i].reshape(nd * GROUP, 8, 128) for i in range(2))
                below, above = neighbours(w)
                v = (v + jnp.where(even_rows(w.shape), -below, above)) * has
                part[c + e, :, :, p] = v.reshape(nd, GROUP, 8, 128)
            return 0

        lax.fori_loop(0, parents, pick, 0)

    def add(c, d, slot):
        def body(k, _):
            part[c, d, k] = part[c, d, k] + ar[c, slot, k]
            return 0

        lax.fori_loop(0, GROUP, body, 0)

    def send_end(c, j):
        @pl.when(z == 0)
        def _():
            right_copy(c, nd - 1 - j).start()

        @pl.when(z == nd - 1)
        def _():
            left_copy(c, j).start()

    def hop(c, t):
        d, k = nd - 1 + z - t, t - (nd - 1 - z)

        @pl.when(jnp.logical_and(z > 0, t >= z))
        def _():
            up_wait(c, d).wait_recv()
            add(c, d, d)
            right_copy(c, d).start()

        @pl.when(jnp.logical_and(z < nd - 1, k >= 0))
        def _():
            up_wait(c, k).wait_recv()
            add(c, k, k)
            left_copy(c, k).start()

    def finish_up(c):
        @pl.when(z > 0)
        def _():
            up_wait(c, z).wait_recv()
            add(c, z, z)

        @pl.when(z < nd - 1)
        def _():
            up_wait(c, nd).wait_recv()
            add(c, z, nd)

        for j in range(1, nb):
            q_copy(c, j).start()
        qa[c, b] = part[c, z, g]

    started = []

    def translate(c):
        if not started:
            started.append(c)
            for j in range(1, GROUP):
                far_copy(j).wait_recv()
            move = pltpu.make_async_copy(farr, fars, sem_fs)
            move.start()
            move.wait()
            for i in range(C):
                trans_copy(i).wait()
        for j in range(1, nb):
            q_copy(c, j).wait_recv()

        def stage(s, _):
            v = qa[c, s]
            below, above = neighbours(v)
            ql[pl.ds(s * parents, parents), 0] = v
            ql[pl.ds(s * parents, parents), 1] = jnp.where(even_rows(v.shape), below, above)
            return 0

        lax.fori_loop(0, nb, stage, 0)
        even = even_rows((8, 128))
        for jg in range(GROUP):

            def body(p, _):
                u = w = None
                for l in range(many):
                    code = fars[jg, p, l]
                    f, kind = code & ((1 << bits) - 1), code >> bits
                    a = trans[c, kind]
                    r, i = a * ql[f, 0], a * ql[f, 1]
                    u = r if u is None else u + r
                    w = i if w is None else w + i
                re = u - pltpu.roll(u, 7, 0)
                im = w + pltpu.roll(w, 1, 0)
                ts[c, jg, p] = jnp.where(even, re, im)
                return 0

            lax.fori_loop(0, parents, body, 0)
        for j in range(1, GROUP):
            t_copy(c, j).start()
        ta[c, g] = ts[c, g]

    def coarse(c):
        for j in range(1, GROUP):
            t_copy(c, j).wait_recv()

        def body(p, _):
            rows = pl.ds(c * GROUP * 8, GROUP * 8)
            v = ta[c, :, p] + upper_ref[p, rows, :].reshape(GROUP, 8, 128)
            coarse_ref[p, rows, :] = v.reshape(GROUP * 8, 128)
            cg[c, z, :, p] = v
            return 0

        lax.fori_loop(0, parents, body, 0)

        @pl.when(z < nd - 1)
        def _():
            down_right(c, z).start()

        @pl.when(z > 0)
        def _():
            down_left(c, z).start()

    def pass_down(c, k):
        @pl.when(jnp.logical_and(z >= k, z < nd - 1))
        def _():
            down_right(c, z - k).wait_recv()
            down_right(c, z - k).start()

        @pl.when(jnp.logical_and(z + k < nd, z > 0))
        def _():
            down_left(c, z + k).wait_recv()
            down_left(c, z + k).start()

    spread = []

    def disaggregate(c):
        @pl.when(z == 0)
        def _():
            for d in range(1, nd):
                down_left(c, d).wait_recv()

        @pl.when(z == nd - 1)
        def _():
            for d in range(nd - 1):
                down_right(c, d).wait_recv()

        spread_map_back(c)

        def stage(p, _):
            v = cg[c, :, :, p].reshape(nd * GROUP, 8, 128)
            below, above = neighbours(v)
            xl[p] = v.reshape(R, 128)
            kl[p] = jnp.where(even_rows(v.shape), below, -above).reshape(R, 128)
            return 0

        lax.fori_loop(0, parents, stage, 0)
        spread.append(c)
        first, last = len(spread) == 1, len(spread) == C
        phi = split(phi_ref[...]) if last else None

        def body(ii, _):
            ys = []
            for q in range(2):
                p, o = itab[PARENT, 2 * ii + q], itab[OCTANT, 2 * ii + q]
                ys.append(cc[c, o] * xl[p] + cs[c, o] * kl[p])
            hi, lo = split(jnp.concatenate(ys, axis=1))
            v = d32(tth[...], jnp.concatenate([hi, lo, hi], axis=0))
            for q in range(2):
                w = v[:, q * 128 : (q + 1) * 128]
                if not first:
                    w = w + fa[2 * ii + q]
                if not last:
                    fa[2 * ii + q] = w
                else:
                    half = w.shape[0] // 2
                    line = jnp.concatenate([w[:half], w[half:]], axis=1)
                    fine_ref[2 * ii + q] = dot3(split(line), phi, turned=True)
            return 0

        lax.fori_loop(0, n // 2, body, 0)

    masks()
    lax.fori_loop(0, n // many_children, along, 0)
    for c in range(C):
        phases_on(c)
    to_scalars.wait()

    def steps(c):
        yield functools.partial(aggregate, c)
        for j in range(nd - 1):
            yield functools.partial(send_end, c, j)
        for t in range(1, nd - 1):
            yield functools.partial(hop, c, t)
        yield functools.partial(finish_up, c)
        yield functools.partial(translate, c)
        yield functools.partial(coarse, c)
        for k in range(1, nd - 1):
            yield functools.partial(pass_down, c, k)
        yield functools.partial(disaggregate, c)

    each = [list(steps(c)) for c in range(C)]
    apart = len(each[0]) // 2
    order = ORDERS.get((nd, C)) or [
        c for _, c in sorted((c * apart + i, c) for c in range(C) for i in range(len(each[c])))
    ]
    for c in order:
        each[c].pop(0)()

    for j in range(1, GROUP):
        far_copy(j).wait_send()

    def drain(c, _):
        for j in range(1, nd):
            zp_copy(c, j).wait_send()
        for j in range(1, nb):
            pf_copy(c, j).wait_send()
            q_copy(c, j).wait_send()
        for j in range(1, GROUP):
            t_copy(c, j).wait_send()
        for d in range(nd):

            @pl.when(d > z)
            def _():
                right_copy(c, d).wait_send()

            @pl.when(d < z)
            def _():
                left_copy(c, d).wait_send()

            @pl.when(jnp.logical_and(d <= z, z < nd - 1))
            def _():
                down_right(c, d).wait_send()

            @pl.when(jnp.logical_and(d >= z, z > 0))
            def _():
                down_left(c, d).wait_send()

        return 0

    lax.fori_loop(0, C, drain, 0)


def shards(
    fine_out,
    theta_interp,
    phi_interp,
    shift_phase,
    translation,
    upper_in,
    children,
    far_boxes,
    far_offsets,
):
    n = fine_out.shape[0]
    tc, tf = theta_interp.shape
    pf_, pc = phi_interp.shape
    parents, many = far_boxes.shape
    nb, nd = lax.axis_size("box"), lax.axis_size("dir")
    noff = translation.shape[0]
    tl = tc // nd
    ROWS = nb // FINE
    GROUP = ROWS // 2
    C = tl // ROWS
    R = nd * GROUP * 8
    PAIR = pair_of(R, C)
    bits = (nb * parents - 1).bit_length()

    phases = (
        shift_phase.reshape(OCT, C, ROWS * 2, 128).transpose(1, 0, 2, 3).reshape(C, OCT * ROWS * 2, 128)
    )

    vmem, smem, hbm = (
        pl.BlockSpec(memory_space=m) for m in (pltpu.VMEM, pltpu.SMEM, pl.ANY)
    )
    dma = pltpu.SemaphoreType.DMA
    tile = (GROUP, parents, 8, 128)
    rows, fine_rows = C * GROUP * 8, tf * 2
    coarse_in, fine_in = pl.pallas_call(
        functools.partial(kernel, (nb, nd, C, ROWS, n, parents, many, bits)),
        in_specs=[smem] + [vmem] * 7 + [hbm],
        out_specs=[vmem, vmem],
        out_shape=[
            jax.ShapeDtypeStruct((parents, rows, 128), F32),
            jax.ShapeDtypeStruct((n, fine_rows, pf_), F32),
        ],
        scratch_shapes=[
            pltpu.VMEM((C, noff, 8, 128), F32),
            pltpu.VMEM((8, 128), I32),
            pltpu.SMEM((8, 128), I32),
            pltpu.VMEM((GROUP, parents, 128), I32),
            pltpu.SMEM((GROUP, parents, 128), I32),
            pltpu.VMEM((C, nd, OCT * 2 * ROWS // nb, 128), F32),
            pltpu.VMEM((C, nb, nd, OCT * 2 * ROWS // nb, 128), F32),
            pltpu.VMEM((C, OCT, R, 128), F32),
            pltpu.VMEM((C, OCT, R, 128), F32),
            pltpu.VMEM((n, 2 * fine_rows, 128), BF16),
            pltpu.VMEM((n, 2 * fine_rows, 128), BF16),
            pltpu.VMEM((PAIR * R, 4 * tf), BF16),
            pltpu.VMEM((PAIR * R, 4 * tf), BF16),
            pltpu.VMEM((4 * tf, 3 * R), BF16),
            pltpu.VMEM((2, tc, 4 * tf), BF16),
            pltpu.VMEM((2, 4 * tf, tc), BF16),
            pltpu.VMEM((PAIR * R, 4 * tf), BF16),
            pltpu.VMEM((4 * tf, R), BF16),
            pltpu.VMEM((n, 2 * PAIR, R, 128), F32),
            pltpu.VMEM((C, nd) + tile, F32),
            pltpu.VMEM((C, nd + 1) + tile, F32),
            pltpu.VMEM((C, nb) + tile[1:], F32),
            pltpu.VMEM((nb * parents, 2, 8, 128), F32),
            pltpu.VMEM((C,) + tile, F32),
            pltpu.VMEM((C,) + tile, F32),
            pltpu.VMEM((C, nd) + tile, F32),
            pltpu.VMEM((parents, R, 128), F32),
            pltpu.VMEM((parents, R, 128), F32),
            pltpu.VMEM((n, 4 * tf, 128), F32),
            dma((C,)),
            dma,
            dma,
            dma((GROUP,)),
            dma((GROUP,)),
            dma((C, nd)),
            dma((C, nd)),
            dma((C, nb)),
            dma((C, nb)),
            dma((C, nd)),
            dma((C, nd + 1)),
            dma((C, nb)),
            dma((C, nb)),
            dma((C, GROUP)),
            dma((C, GROUP)),
            dma((C, nd)),
            dma((C, nd)),
            dma((C, nd)),
        ],
        compiler_params=pltpu.CompilerParams(
            collective_id=0, has_side_effects=True, vmem_limit_bytes=VMEM_BYTES
        ),
    )(
        children.T,
        far_boxes,
        far_offsets,
        phases,
        rows_view(fine_out),
        phi_interp,
        theta_interp.T,
        rows_view(upper_in),
        rows_view(translation),
    )
    return rows_unview(coarse_in), rows_unview(fine_in)


def solution(mesh):
    placed = (
        P(("box", "dir"), None, None),
        P(),
        P(),
        P(None, "dir"),
        P(None, None, "dir"),
        P("box", None, "dir"),
        P("box", None),
        P("box", None),
        P("box", None),
    )
    return jax.shard_map(
        shards,
        mesh=mesh,
        in_specs=placed,
        out_specs=(P("box", None, "dir"), P(("box", "dir"), None, None)),
        check_vma=False,
    )
```

```python
import functools

import jax
import jax.numpy as jnp
from jax import lax
from jax.experimental import pallas as pl
from jax.experimental.pallas import tpu as pltpu
from jax.sharding import PartitionSpec as P

F32, BF16, I32 = jnp.float32, jnp.bfloat16, jnp.int32
MESH = pl.DeviceIdType.MESH
VMEM_BYTES = 60 * 1024 * 1024
FINE = 2
ORDERS = {
    (4, 8): (0, 0, 0, 0, 1, 1, 7, 0, 7, 1, 7, 2, 0, 2, 5, 3, 7, 1, 7, 2, 0, 5, 1, 5, 7, 3, 2, 2, 5, 0, 1, 7, 2, 1, 5, 4, 0, 3, 7, 6, 3, 3, 5, 1, 4, 2, 7, 4, 1, 0, 3, 2, 4, 5, 0, 6, 4, 2, 7, 3, 0, 4, 6, 1, 5, 6, 7, 3, 6, 5, 2, 4, 7, 6, 3, 2, 5, 4, 6, 4, 5, 3, 2, 4, 6, 3, 1, 5, 6, 1, 4, 3, 6, 4, 6, 6),
    (4, 4): (2, 2, 0, 0, 2, 0, 1, 2, 0, 1, 0, 2, 0, 2, 3, 0, 1, 3, 1, 1, 2, 0, 3, 1, 3, 2, 3, 0, 2, 1, 3, 1, 0, 1, 3, 2, 0, 3, 1, 2, 3, 1, 0, 2, 3, 1, 3, 3),
}
OCT = 8

COS = (
    0.999999999880854,
    -0.49999999845758136,
    0.04166666339221376,
    -0.001388886238622854,
    2.48005323812661e-05,
    -2.753445728365435e-07,
    2.0600835499376906e-09,
    -9.713911649043148e-12,
)
SIN = (
    0.9999999992304494,
    -0.166666659035747,
    0.008333320978968734,
    -0.00019840518737424315,
    2.7535517055355563e-06,
    -2.4725519533129986e-08,
    1.360099414116501e-10,
)


def split(x):
    hi = x.astype(BF16)
    return hi, (x - hi.astype(F32)).astype(BF16)


def dot3(a, b, turned=False):
    (ah, al), (bh, bl) = a, b
    sums = (((1,), (1 if turned else 0,)), ((), ()))
    d = functools.partial(lax.dot_general, dimension_numbers=sums, preferred_element_type=F32)
    return d(ah, bh) + (d(ah, bl) + d(al, bh))


def horner(y, coefficients):
    r = jnp.full_like(y, coefficients[-1])
    for c in coefficients[-2::-1]:
        r = r * y + c
    return r


def pair_of(rows, chunks):
    return 2 if rows <= 64 and chunks % 2 == 0 else 1


def rows_view(x):
    n, _, k = x.shape
    return x.reshape(n, 2, k // 128, 128).transpose(0, 2, 1, 3).reshape(n, k // 64, 128)


def rows_unview(x):
    n, r, _ = x.shape
    return x.reshape(n, r // 2, 2, 128).transpose(0, 2, 1, 3).reshape(n, 2, r * 64)


def neighbours(v):
    return pltpu.roll(v, 7, v.ndim - 2), pltpu.roll(v, 1, v.ndim - 2)


def even_rows(shape):
    return lax.broadcasted_iota(I32, shape, len(shape) - 2) % 2 == 0


def kernel(
    dims,
    children_ref,
    boxes_ref,
    kinds_ref,
    phase_ref,
    x_hbm,
    phi_ref,
    thetat_ref,
    upper_hbm,
    trans_ref,
    coarse_ref,
    fine_ref,
    x_ref,
    upper_ref,
    trans,
    tabv,
    itab,
    farr,
    fars,
    zp,
    pf,
    cc,
    cs,
    flat,
    alh,
    all_,
    th,
    tl_,
    tth,
    wide,
    widet,
    mask,
    maskt,
    sb,
    part,
    ar,
    qa,
    ql,
    ts,
    ta,
    cg,
    xl,
    kl,
    fa,
    sem_x,
    sem_u,
    sem_tr,
    sem_fs,
    sem_tab,
    far_s,
    far_r,
    zp_s,
    zp_r,
    pf_s,
    pf_r,
    up_s,
    up_r,
    q_s,
    q_r,
    t_s,
    t_r,
    dr_s,
    dl_s,
    d_r,
):
    nb, nd, C, ROWS, n, parents, many = dims
    GROUP = ROWS // 2
    PER = GROUP * 8
    R = nd * PER
    PAIR = pair_of(R, C)
    b, z = lax.axis_index("box"), lax.axis_index("dir")
    g, h = b % GROUP, b // GROUP
    own_tiles = 2 * ROWS // nb
    PERM, OCTS, PARENT, OCTANT, LAST, KEEP, HAS = range(7)

    def remote(src, dst, ss, rs, dev):
        return pltpu.make_async_remote_copy(
            src_ref=src, dst_ref=dst, send_sem=ss, recv_sem=rs, device_id=dev, device_id_type=MESH
        )

    def zp_copy(c, j):
        to = (z + j) % nd
        return remote(
            phase_ref.at[pl.ds(c * 2 * ROWS + b * own_tiles, own_tiles)],
            zp.at[c, z],
            zp_s.at[c, j],
            zp_r.at[c, j],
            (b, to),
        )

    def pf_copy(c, j):
        return remote(zp.at[c], pf.at[c, b], pf_s.at[c, j], pf_r.at[c, j], (b ^ j, z))

    def far_copy(j):
        return remote(farr.at[g], farr.at[g], far_s.at[j], far_r.at[j], (b ^ j, z))

    def right_copy(c, d):
        return remote(part.at[c, d], ar.at[c, d], up_s.at[c, d], up_r.at[c, d], (b, z + 1))

    def left_copy(c, d):
        slot = jnp.where(z - 1 == d, nd, d)
        return remote(part.at[c, d], ar.at[c, slot], up_s.at[c, d], up_r.at[c, slot], (b, z - 1))

    def up_wait(c, slot):
        return remote(part.at[c, 0], ar.at[c, slot], up_s.at[c, 0], up_r.at[c, slot], (b, z))

    def q_copy(c, j):
        to = b ^ j
        return remote(
            part.at[c, z, to % GROUP], qa.at[c, b], q_s.at[c, j], q_r.at[c, j], (to, z)
        )

    def t_copy(c, j):
        return remote(ts.at[c, g ^ j], ta.at[c, g], t_s.at[c, j], t_r.at[c, j], (b ^ j, z))

    def down_right(c, d):
        return remote(cg.at[c, d], cg.at[c, d], dr_s.at[c, d], d_r.at[c, d], (b, z + 1))

    def down_left(c, d):
        return remote(cg.at[c, d], cg.at[c, d], dl_s.at[c, d], d_r.at[c, d], (b, z - 1))

    def trans_copy(c):
        row = pl.multiple_of((c * GROUP + g) * 8, 8)
        return pltpu.make_async_copy(trans_ref.at[:, pl.ds(row, 8)], trans.at[c], sem_tr.at[c])

    x_in = pltpu.make_async_copy(x_hbm, x_ref, sem_x)
    upper_in = pltpu.make_async_copy(upper_hbm, upper_ref, sem_u)
    x_in.start()
    upper_in.start()
    for c in range(C):
        trans_copy(c).start()

    farr[g, :, 0:many] = boxes_ref[...]
    farr[g, :, 64 : 64 + many] = kinds_ref[...]
    barrier = pltpu.get_barrier_semaphore()
    for j in range(1, nb):
        pl.semaphore_signal(barrier, inc=1, device_id=(b ^ j, z), device_id_type=MESH)
    for j in range(1, nd):
        pl.semaphore_signal(barrier, inc=1, device_id=(b, (z + j) % nd), device_id_type=MESH)
    pl.semaphore_wait(barrier, nb + nd - 2)

    for c in range(C):
        for j in range(1, nd):
            zp_copy(c, j).start()
    for j in range(1, GROUP):
        far_copy(j).start()
    for c in range(C):
        zp[c, z] = phase_ref[pl.ds(c * 2 * ROWS + b * own_tiles, own_tiles)]

    lanes = lax.broadcasted_iota(I32, (1, 128), 1)

    def table(p, carry):
        k, rows = carry[0], list(carry[1:])
        first = k
        for o in range(OCT):
            local = lax.rem(children_ref[o, p], n * nd) - z * n
            own = jnp.logical_and(local >= 0, local < n)
            here, at = lanes == jnp.where(own, k, -1), lanes == jnp.where(own, local, -1)
            rows[PERM] = jnp.where(here, local, rows[PERM])
            rows[OCTS] = jnp.where(here, o, rows[OCTS])
            rows[KEEP] = jnp.where(here, jnp.where(k > first, 1, 0), rows[KEEP])
            rows[PARENT] = jnp.where(at, p, rows[PARENT])
            rows[OCTANT] = jnp.where(at, o, rows[OCTANT])
            k = k + jnp.where(own, 1, 0)
        rows[LAST] = jnp.where(lanes == p, jnp.clip(k - 1, 0, n - 1), rows[LAST])
        rows[HAS] = jnp.where(lanes == p, jnp.where(k > first, 1, 0), rows[HAS])
        return (k, *rows)

    none = jnp.zeros((1, 128), I32)
    found = lax.fori_loop(0, parents, table, (jnp.int32(0), *[none] * 7))
    for i in range(7):
        tabv[i : i + 1, :] = found[1 + i]
    tabv[7:8, :] = none
    to_scalars = pltpu.make_async_copy(tabv, itab, sem_tab)
    to_scalars.start()

    phi = split(phi_ref[...])
    many_children = 4

    def along(i, _):
        rows = x_ref.shape[1]
        v = x_ref[pl.ds(i * many_children, many_children)].reshape(many_children * rows, 128)
        y = dot3(split(v), phi)
        for q in range(many_children):
            for half in range(2):
                hi, lo = split(y[q * rows : (q + 1) * rows, half * 128 : (half + 1) * 128])
                alh[i * many_children + q, half * rows : (half + 1) * rows, :] = hi
                all_[i * many_children + q, half * rows : (half + 1) * rows, :] = lo
        return 0

    def phases_on(c):
        for j in range(1, nd):
            zp_copy(c, j).wait_recv()
        for j in range(1, nb):
            pf_copy(c, j).start()
        pf[c, b] = zp[c]

    def shifts(c):
        for j in range(1, nb):
            pf_copy(c, j).wait_recv()
        def body(i, _):
            for d in range(nd):
                for j in range(own_tiles):
                    v = pf[c, i, d, j]
                    y = v * v
                    co, si = horner(y, COS), v * horner(y, SIN)
                    for p in range(2):
                        row = d * PER + 2 * (i * own_tiles + j) + p
                        flat[0, pl.ds(row, OCT, stride=R), :] = co
                        flat[1, pl.ds(row, OCT, stride=R), :] = si
            return 0

        lax.fori_loop(0, nb, body, 0)

        def place(o, _):
            rows = pl.ds(pl.multiple_of(o * R, 8), R)
            cc[c, o] = flat[0, rows, :]
            cs[c, o] = flat[1, rows, :]
            return 0

        lax.fori_loop(0, OCT, place, 0)

    def turn(c, o):
        return cc[c, o], cs[c, o]

    tf, tc = thetat_ref.shape
    tl = tc // nd

    def axis(shape, d):
        return lax.broadcasted_iota(I32, shape, d)

    def ones(shape, hit):
        return jnp.where(hit, 1.0, 0.0).astype(BF16)

    def fine_row(i):
        return (i >> 1) & (tf - 1)

    def polar_row(c, r):
        c, r = c + (r >> (R.bit_length() - 1)), r & (R - 1)
        return (r >> (PER.bit_length() - 1)) * tl + c * ROWS + ((r >> 2) & (ROWS - 1))

    def masks():
        shape = (PAIR * R, 4 * tf)
        r, k = axis(shape, 0), axis(shape, 1)
        hit = (((r >> 1) & 1) == jnp.where(k >= 2 * tf, 1, 0)) & ((r & 1) == (k & 1))
        mask[...] = ones(shape, hit)
        shape = (4 * tf, R)
        k, r = axis(shape, 0), axis(shape, 1)
        hit = (((r >> 1) & 1) == jnp.where(k >= 2 * tf, 1, 0)) & ((r & 1) == (k & 1))
        maskt[...] = ones(shape, hit)
        shape = (tf, 4 * tf)
        w = ones(shape, fine_row(axis(shape, 1)) == axis(shape, 0))
        shape = (4 * tf, tf)
        wt = ones(shape, fine_row(axis(shape, 0)) == axis(shape, 1))
        for v, out in zip(split(thetat_ref[...].T), (0, 1)):
            wide[out] = d32(v, w).astype(BF16)
        for v, out in zip(split(thetat_ref[...]), (0, 1)):
            widet[out] = d32(wt, v).astype(BF16)

    d32 = functools.partial(jnp.dot, preferred_element_type=F32)

    def spread_map(c):
        shape = (PAIR * R, tc)
        pick = ones(shape, polar_row(c, axis(shape, 0)) == axis(shape, 1))
        for i, out in enumerate((th, tl_)):
            out[...] = d32(pick, wide[i]).astype(BF16) * mask[...]

    def spread_map_back(c):
        shape = (tc, R)
        pick = ones(shape, polar_row(c, axis(shape, 1)) == axis(shape, 0))
        for i, source in enumerate((0, 0, 1)):
            tth[:, i * R : (i + 1) * R] = d32(widet[source], pick).astype(BF16) * maskt[...]

    gathered = set()

    def aggregate(c):
        c = c // PAIR * PAIR
        if c in gathered:
            return
        gathered.add(c)
        for e in range(PAIR):
            shifts(c + e)
        spread_map(c)

        def body(kk, sums):
            k = 2 * kk
            i0, i1 = itab[PERM, k], itab[PERM, k + 1]
            rh = jnp.concatenate([alh[i0], alh[i1]], axis=1)
            rl = jnp.concatenate([all_[i0], all_[i1]], axis=1)
            v = dot3((th[...], tl_[...]), (rh, rl))
            for q in range(2):
                o, keep = itab[OCTS, k + q], itab[KEEP, k + q].astype(F32)
                for e in range(PAIR):
                    w = v[e * R : (e + 1) * R, q * 128 : (q + 1) * 128]
                    for i, m in enumerate(turn(c + e, o)):
                        sums[2 * e + i] = sums[2 * e + i] * keep + m * w
                for e in range(2 * PAIR):
                    sb[k + q, e] = sums[e]
            return sums

        lax.fori_loop(0, n // 2, body, [jnp.zeros((R, 128), F32)] * (2 * PAIR))

        def pick(p, _):
            last, has = itab[LAST, p], itab[HAS, p].astype(F32)
            for e in range(PAIR):
                v, w = (sb[last, 2 * e + i].reshape(nd * GROUP, 8, 128) for i in range(2))
                below, above = neighbours(w)
                v = (v + jnp.where(even_rows(w.shape), -below, above)) * has
                part[c + e, :, :, p] = v.reshape(nd, GROUP, 8, 128)
            return 0

        lax.fori_loop(0, parents, pick, 0)

    def add(c, d, slot):
        def body(k, _):
            part[c, d, k] = part[c, d, k] + ar[c, slot, k]
            return 0

        lax.fori_loop(0, GROUP, body, 0)

    def send_end(c, j):
        @pl.when(z == 0)
        def _():
            right_copy(c, nd - 1 - j).start()

        @pl.when(z == nd - 1)
        def _():
            left_copy(c, j).start()

    def hop(c, t):
        d, k = nd - 1 + z - t, t - (nd - 1 - z)

        @pl.when(jnp.logical_and(z > 0, t >= z))
        def _():
            up_wait(c, d).wait_recv()
            add(c, d, d)
            right_copy(c, d).start()

        @pl.when(jnp.logical_and(z < nd - 1, k >= 0))
        def _():
            up_wait(c, k).wait_recv()
            add(c, k, k)
            left_copy(c, k).start()

    def finish_up(c):
        @pl.when(z > 0)
        def _():
            up_wait(c, z).wait_recv()
            add(c, z, z)

        @pl.when(z < nd - 1)
        def _():
            up_wait(c, nd).wait_recv()
            add(c, z, nd)

        for j in range(1, nb):
            q_copy(c, j).start()
        qa[c, b] = part[c, z, g]

    started = []

    def translate(c):
        if not started:
            started.append(c)
            for j in range(1, GROUP):
                far_copy(j).wait_recv()
            move = pltpu.make_async_copy(farr, fars, sem_fs)
            move.start()
            move.wait()
            for i in range(C):
                trans_copy(i).wait()
        for j in range(1, nb):
            q_copy(c, j).wait_recv()

        def stage(s, _):
            v = qa[c, s]
            below, above = neighbours(v)
            ql[pl.ds(s * parents, parents), 0] = v
            ql[pl.ds(s * parents, parents), 1] = jnp.where(even_rows(v.shape), below, above)
            return 0

        lax.fori_loop(0, nb, stage, 0)
        even = even_rows((8, 128))
        for jg in range(GROUP):

            def body(p, _):
                u = w = None
                for l in range(many):
                    f, kind = fars[jg, p, l], fars[jg, p, 64 + l]
                    a = trans[c, kind]
                    r, i = a * ql[f, 0], a * ql[f, 1]
                    u = r if u is None else u + r
                    w = i if w is None else w + i
                re = u - pltpu.roll(u, 7, 0)
                im = w + pltpu.roll(w, 1, 0)
                ts[c, jg, p] = jnp.where(even, re, im)
                return 0

            lax.fori_loop(0, parents, body, 0)
        for j in range(1, GROUP):
            t_copy(c, j).start()
        ta[c, g] = ts[c, g]

    def coarse(c):
        for j in range(1, GROUP):
            t_copy(c, j).wait_recv()

        def body(p, _):
            rows = pl.ds(c * GROUP * 8, GROUP * 8)
            v = ta[c, :, p] + upper_ref[p, rows, :].reshape(GROUP, 8, 128)
            coarse_ref[p, rows, :] = v.reshape(GROUP * 8, 128)
            cg[c, z, :, p] = v
            return 0

        lax.fori_loop(0, parents, body, 0)

        @pl.when(z < nd - 1)
        def _():
            down_right(c, z).start()

        @pl.when(z > 0)
        def _():
            down_left(c, z).start()

    def pass_down(c, k):
        @pl.when(jnp.logical_and(z >= k, z < nd - 1))
        def _():
            down_right(c, z - k).wait_recv()
            down_right(c, z - k).start()

        @pl.when(jnp.logical_and(z + k < nd, z > 0))
        def _():
            down_left(c, z + k).wait_recv()
            down_left(c, z + k).start()

    spread = []

    def disaggregate(c):
        @pl.when(z == 0)
        def _():
            for d in range(1, nd):
                down_left(c, d).wait_recv()

        @pl.when(z == nd - 1)
        def _():
            for d in range(nd - 1):
                down_right(c, d).wait_recv()

        spread_map_back(c)

        def stage(p, _):
            v = cg[c, :, :, p].reshape(nd * GROUP, 8, 128)
            below, above = neighbours(v)
            xl[p] = v.reshape(R, 128)
            kl[p] = jnp.where(even_rows(v.shape), below, -above).reshape(R, 128)
            return 0

        lax.fori_loop(0, parents, stage, 0)
        spread.append(c)
        first, last = len(spread) == 1, len(spread) == C
        phi = split(phi_ref[...]) if last else None

        def pair(i):
            ys = []
            for q in range(2):
                p, o = itab[PARENT, i + q], itab[OCTANT, i + q]
                co, si = turn(c, o)
                ys.append(co * xl[p] + si * kl[p])
            hi, lo = split(jnp.concatenate(ys, axis=1))
            return d32(tth[...], jnp.concatenate([hi, lo, hi], axis=0))

        def body(ii, _):
            pairs = [pair(4 * ii), pair(4 * ii + 2)]
            for q in range(4):
                i = 4 * ii + q
                w = pairs[q // 2][:, q % 2 * 128 : (q % 2 + 1) * 128]
                if not first:
                    w = w + fa[i]
                if not last:
                    fa[i] = w
                else:
                    half = w.shape[0] // 2
                    line = jnp.concatenate([w[:half], w[half:]], axis=1)
                    fine_ref[i] = dot3(split(line), phi, turned=True)
            return 0

        lax.fori_loop(0, n // 4, body, 0)

    masks()
    for c in range(C):
        phases_on(c)
    x_in.wait()
    lax.fori_loop(0, n // many_children, along, 0)
    to_scalars.wait()
    upper_in.wait()

    def steps(c):
        yield functools.partial(aggregate, c)
        for j in range(nd - 1):
            yield functools.partial(send_end, c, j)
        for t in range(1, nd - 1):
            yield functools.partial(hop, c, t)
        yield functools.partial(finish_up, c)
        yield functools.partial(translate, c)
        yield functools.partial(coarse, c)
        for k in range(1, nd - 1):
            yield functools.partial(pass_down, c, k)
        yield functools.partial(disaggregate, c)

    each = [list(steps(c)) for c in range(C)]
    apart = len(each[0]) // 2
    order = ORDERS.get((nd, C)) or [
        c for _, c in sorted((c * apart + i, c) for c in range(C) for i in range(len(each[c])))
    ]
    for c in order:
        each[c].pop(0)()

    for j in range(1, GROUP):
        far_copy(j).wait_send()

    def drain(c, _):
        for j in range(1, nd):
            zp_copy(c, j).wait_send()
        for j in range(1, nb):
            pf_copy(c, j).wait_send()
            q_copy(c, j).wait_send()
        for j in range(1, GROUP):
            t_copy(c, j).wait_send()
        for d in range(nd):

            @pl.when(d > z)
            def _():
                right_copy(c, d).wait_send()

            @pl.when(d < z)
            def _():
                left_copy(c, d).wait_send()

            @pl.when(jnp.logical_and(d <= z, z < nd - 1))
            def _():
                down_right(c, d).wait_send()

            @pl.when(jnp.logical_and(d >= z, z > 0))
            def _():
                down_left(c, d).wait_send()

        return 0

    lax.fori_loop(0, C, drain, 0)


def shards(
    fine_out,
    theta_interp,
    phi_interp,
    shift_phase,
    translation,
    upper_in,
    children,
    far_boxes,
    far_offsets,
):
    n = fine_out.shape[0]
    tc, tf = theta_interp.shape
    pf_, pc = phi_interp.shape
    parents, many = far_boxes.shape
    nb, nd = lax.axis_size("box"), lax.axis_size("dir")
    noff = translation.shape[0]
    tl = tc // nd
    ROWS = nb // FINE
    GROUP = ROWS // 2
    C = tl // ROWS
    R = nd * GROUP * 8
    PAIR = pair_of(R, C)

    phases = shift_phase.reshape(OCT, tl * 2, 128).transpose(1, 0, 2)

    vmem, smem, hbm = (
        pl.BlockSpec(memory_space=m) for m in (pltpu.VMEM, pltpu.SMEM, pl.ANY)
    )
    dma = pltpu.SemaphoreType.DMA
    tile = (GROUP, parents, 8, 128)
    rows, fine_rows = C * GROUP * 8, tf * 2
    coarse_in, fine_in = pl.pallas_call(
        functools.partial(kernel, (nb, nd, C, ROWS, n, parents, many)),
        in_specs=[smem] + [vmem] * 3 + [hbm] + [vmem] * 2 + [hbm] * 2,
        out_specs=[vmem, vmem],
        out_shape=[
            jax.ShapeDtypeStruct((parents, rows, 128), F32),
            jax.ShapeDtypeStruct((n, fine_rows, pf_), F32),
        ],
        scratch_shapes=[
            pltpu.VMEM((n, fine_rows, pf_), F32),
            pltpu.VMEM((parents, rows, 128), F32),
            pltpu.VMEM((C, noff, 8, 128), F32),
            pltpu.VMEM((8, 128), I32),
            pltpu.SMEM((8, 128), I32),
            pltpu.VMEM((GROUP, parents, 128), I32),
            pltpu.SMEM((GROUP, parents, 128), I32),
            pltpu.VMEM((C, nd, 2 * ROWS // nb, OCT, 128), F32),
            pltpu.VMEM((C, nb, nd, 2 * ROWS // nb, OCT, 128), F32),
            pltpu.VMEM((C, OCT, R, 128), F32),
            pltpu.VMEM((C, OCT, R, 128), F32),
            pltpu.VMEM((2, OCT * R, 128), F32),
            pltpu.VMEM((n, 2 * fine_rows, 128), BF16),
            pltpu.VMEM((n, 2 * fine_rows, 128), BF16),
            pltpu.VMEM((PAIR * R, 4 * tf), BF16),
            pltpu.VMEM((PAIR * R, 4 * tf), BF16),
            pltpu.VMEM((4 * tf, 3 * R), BF16),
            pltpu.VMEM((2, tc, 4 * tf), BF16),
            pltpu.VMEM((2, 4 * tf, tc), BF16),
            pltpu.VMEM((PAIR * R, 4 * tf), BF16),
            pltpu.VMEM((4 * tf, R), BF16),
            pltpu.VMEM((n, 2 * PAIR, R, 128), F32),
            pltpu.VMEM((C, nd) + tile, F32),
            pltpu.VMEM((C, nd + 1) + tile, F32),
            pltpu.VMEM((C, nb) + tile[1:], F32),
            pltpu.VMEM((nb * parents, 2, 8, 128), F32),
            pltpu.VMEM((C,) + tile, F32),
            pltpu.VMEM((C,) + tile, F32),
            pltpu.VMEM((C, nd) + tile, F32),
            pltpu.VMEM((parents, R, 128), F32),
            pltpu.VMEM((parents, R, 128), F32),
            pltpu.VMEM((n, 4 * tf, 128), F32),
            dma,
            dma,
            dma((C,)),
            dma,
            dma,
            dma((GROUP,)),
            dma((GROUP,)),
            dma((C, nd)),
            dma((C, nd)),
            dma((C, nb)),
            dma((C, nb)),
            dma((C, nd)),
            dma((C, nd + 1)),
            dma((C, nb)),
            dma((C, nb)),
            dma((C, GROUP)),
            dma((C, GROUP)),
            dma((C, nd)),
            dma((C, nd)),
            dma((C, nd)),
        ],
        compiler_params=pltpu.CompilerParams(
            collective_id=0, has_side_effects=True, vmem_limit_bytes=VMEM_BYTES
        ),
    )(
        children.T,
        far_boxes,
        far_offsets,
        phases,
        rows_view(fine_out),
        phi_interp,
        theta_interp.T,
        rows_view(upper_in),
        rows_view(translation),
    )
    return rows_unview(coarse_in), rows_unview(fine_in)


def solution(mesh):
    placed = (
        P(("box", "dir"), None, None),
        P(),
        P(),
        P(None, "dir"),
        P(None, None, "dir"),
        P("box", None, "dir"),
        P("box", None),
        P("box", None),
        P("box", None),
    )
    return jax.shard_map(
        shards,
        mesh=mesh,
        in_specs=placed,
        out_specs=(P("box", None, "dir"), P(("box", "dir"), None, None)),
        check_vma=False,
    )
```

```python
import functools

import jax
import jax.numpy as jnp
from jax import lax
from jax.experimental import pallas as pl
from jax.experimental.pallas import tpu as pltpu
from jax.sharding import PartitionSpec as P

F32, BF16, I32 = jnp.float32, jnp.bfloat16, jnp.int32
MESH = pl.DeviceIdType.MESH
VMEM_BYTES = 60 * 1024 * 1024
FINE = 2
ORDERS = {
    (4, 8): (0, 0, 0, 0, 1, 1, 7, 0, 7, 1, 7, 2, 0, 2, 5, 3, 7, 1, 7, 2, 0, 5, 1, 5, 7, 3, 2, 2, 5, 0, 1, 7, 2, 1, 5, 4, 0, 3, 7, 6, 3, 3, 5, 1, 4, 2, 7, 4, 1, 0, 3, 2, 4, 5, 0, 6, 4, 2, 7, 3, 0, 4, 6, 1, 5, 6, 7, 3, 6, 5, 2, 4, 7, 6, 3, 2, 5, 4, 6, 4, 5, 3, 2, 4, 6, 3, 1, 5, 6, 1, 4, 3, 6, 4, 6, 6),
    (4, 4): (2, 2, 0, 0, 2, 0, 1, 2, 0, 1, 0, 2, 0, 2, 3, 0, 1, 3, 1, 1, 2, 0, 3, 1, 3, 2, 3, 0, 2, 1, 3, 1, 0, 1, 3, 2, 0, 3, 1, 2, 3, 1, 0, 2, 3, 1, 3, 3),
}
OCT = 8

COS = (
    0.999999999880854,
    -0.49999999845758136,
    0.04166666339221376,
    -0.001388886238622854,
    2.48005323812661e-05,
    -2.753445728365435e-07,
    2.0600835499376906e-09,
    -9.713911649043148e-12,
)
SIN = (
    0.9999999992304494,
    -0.166666659035747,
    0.008333320978968734,
    -0.00019840518737424315,
    2.7535517055355563e-06,
    -2.4725519533129986e-08,
    1.360099414116501e-10,
)


def split(x):
    hi = x.astype(BF16)
    return hi, (x - hi.astype(F32)).astype(BF16)


def dot3(a, b, turned=False):
    (ah, al), (bh, bl) = a, b
    sums = (((1,), (1 if turned else 0,)), ((), ()))
    d = functools.partial(lax.dot_general, dimension_numbers=sums, preferred_element_type=F32)
    return d(ah, bh) + (d(ah, bl) + d(al, bh))


def horner(y, coefficients):
    r = jnp.full_like(y, coefficients[-1])
    for c in coefficients[-2::-1]:
        r = r * y + c
    return r


def pair_of(rows, chunks):
    return 2 if rows <= 64 and chunks % 2 == 0 else 1


def rows_view(x):
    n, _, k = x.shape
    return x.reshape(n, 2, k // 128, 128).transpose(0, 2, 1, 3).reshape(n, k // 64, 128)


def rows_unview(x):
    n, r, _ = x.shape
    return x.reshape(n, r // 2, 2, 128).transpose(0, 2, 1, 3).reshape(n, 2, r * 64)


def neighbours(v):
    return pltpu.roll(v, 7, v.ndim - 2), pltpu.roll(v, 1, v.ndim - 2)


def even_rows(shape):
    return lax.broadcasted_iota(I32, shape, len(shape) - 2) % 2 == 0


def kernel(
    dims,
    children_ref,
    boxes_ref,
    kinds_ref,
    phase_ref,
    x_hbm,
    phi_ref,
    thetat_ref,
    upper_hbm,
    trans_ref,
    coarse_hbm,
    fine_hbm,
    coarse_ref,
    fine_ref,
    x_ref,
    upper_ref,
    trans,
    tabv,
    itab,
    farr,
    fars,
    zp,
    pf,
    cc,
    cs,
    flat,
    alh,
    all_,
    th,
    tl_,
    tth,
    wide,
    widet,
    mask,
    maskt,
    sb,
    part,
    ar,
    qa,
    ql,
    ts,
    ta,
    cg,
    xl,
    kl,
    fa,
    sem_x,
    sem_u,
    sem_c,
    sem_f,
    sem_tr,
    sem_fs,
    sem_tab,
    far_s,
    far_r,
    zp_s,
    zp_r,
    pf_s,
    pf_r,
    up_s,
    up_r,
    q_s,
    q_r,
    t_s,
    t_r,
    dr_s,
    dl_s,
    d_r,
):
    nb, nd, C, ROWS, n, parents, many = dims
    GROUP = ROWS // 2
    PER = GROUP * 8
    R = nd * PER
    PAIR = pair_of(R, C)
    b, z = lax.axis_index("box"), lax.axis_index("dir")
    g, h = b % GROUP, b // GROUP
    own_tiles = 2 * ROWS // nb
    count = 3 * nd
    order = ORDERS.get((nd, C)) or [
        c for _, c in sorted((c * (count // 2) + i, c) for c in range(C) for i in range(count))
    ]
    PERM, OCTS, PARENT, OCTANT, LAST, KEEP, HAS = range(7)

    def remote(src, dst, ss, rs, dev):
        return pltpu.make_async_remote_copy(
            src_ref=src, dst_ref=dst, send_sem=ss, recv_sem=rs, device_id=dev, device_id_type=MESH
        )

    def zp_copy(c, j):
        to = (z + j) % nd
        return remote(
            phase_ref.at[pl.ds(c * 2 * ROWS + b * own_tiles, own_tiles)],
            zp.at[c, z],
            zp_s.at[c, j],
            zp_r.at[c, j],
            (b, to),
        )

    def pf_copy(c, j):
        return remote(zp.at[c], pf.at[c, b], pf_s.at[c, j], pf_r.at[c, j], (b ^ j, z))

    def far_copy(j):
        return remote(farr.at[g], farr.at[g], far_s.at[j], far_r.at[j], (b ^ j, z))

    def right_copy(c, d):
        return remote(part.at[c, d], ar.at[c, d], up_s.at[c, d], up_r.at[c, d], (b, z + 1))

    def left_copy(c, d):
        slot = jnp.where(z - 1 == d, nd, d)
        return remote(part.at[c, d], ar.at[c, slot], up_s.at[c, d], up_r.at[c, slot], (b, z - 1))

    def up_wait(c, slot):
        return remote(part.at[c, 0], ar.at[c, slot], up_s.at[c, 0], up_r.at[c, slot], (b, z))

    def q_copy(c, j):
        to = b ^ j
        return remote(
            part.at[c, z, to % GROUP], qa.at[c, b], q_s.at[c, j], q_r.at[c, j], (to, z)
        )

    def t_copy(c, j):
        return remote(ts.at[c, g ^ j], ta.at[c, g], t_s.at[c, j], t_r.at[c, j], (b ^ j, z))

    def down_right(c, d):
        return remote(cg.at[c, d], cg.at[c, d], dr_s.at[c, d], d_r.at[c, d], (b, z + 1))

    def down_left(c, d):
        return remote(cg.at[c, d], cg.at[c, d], dl_s.at[c, d], d_r.at[c, d], (b, z - 1))

    def trans_copy(c):
        row = pl.multiple_of((c * GROUP + g) * 8, 8)
        return pltpu.make_async_copy(trans_ref.at[:, pl.ds(row, 8)], trans.at[c], sem_tr.at[c])

    x_in = pltpu.make_async_copy(x_hbm, x_ref, sem_x)
    upper_in = pltpu.make_async_copy(upper_hbm, upper_ref, sem_u)
    x_in.start()
    upper_in.start()
    for c in range(C):
        trans_copy(c).start()

    farr[g, :, 0:many] = boxes_ref[...]
    farr[g, :, 64 : 64 + many] = kinds_ref[...]
    barrier = pltpu.get_barrier_semaphore()
    for j in range(1, nb):
        pl.semaphore_signal(barrier, inc=1, device_id=(b ^ j, z), device_id_type=MESH)
    for j in range(1, nd):
        pl.semaphore_signal(barrier, inc=1, device_id=(b, (z + j) % nd), device_id_type=MESH)
    pl.semaphore_wait(barrier, nb + nd - 2)

    use = [q for p in dict.fromkeys(c // PAIR for c in order) for q in range(p * PAIR, (p + 1) * PAIR)]
    for c in use:
        for j in range(1, nd):
            zp_copy(c, j).start()
    for j in range(1, GROUP):
        far_copy(j).start()
    for c in range(C):
        zp[c, z] = phase_ref[pl.ds(c * 2 * ROWS + b * own_tiles, own_tiles)]

    lanes = lax.broadcasted_iota(I32, (1, 128), 1)

    def table(p, carry):
        k, rows = carry[0], list(carry[1:])
        first = k
        for o in range(OCT):
            local = lax.rem(children_ref[o, p], n * nd) - z * n
            own = jnp.logical_and(local >= 0, local < n)
            here, at = lanes == jnp.where(own, k, -1), lanes == jnp.where(own, local, -1)
            rows[PERM] = jnp.where(here, local, rows[PERM])
            rows[OCTS] = jnp.where(here, o, rows[OCTS])
            rows[KEEP] = jnp.where(here, jnp.where(k > first, 1, 0), rows[KEEP])
            rows[PARENT] = jnp.where(at, p, rows[PARENT])
            rows[OCTANT] = jnp.where(at, o, rows[OCTANT])
            k = k + jnp.where(own, 1, 0)
        rows[LAST] = jnp.where(lanes == p, jnp.clip(k - 1, 0, n - 1), rows[LAST])
        rows[HAS] = jnp.where(lanes == p, jnp.where(k > first, 1, 0), rows[HAS])
        return (k, *rows)

    none = jnp.zeros((1, 128), I32)
    found = lax.fori_loop(0, parents, table, (jnp.int32(0), *[none] * 7))
    for i in range(7):
        tabv[i : i + 1, :] = found[1 + i]
    tabv[7:8, :] = none
    to_scalars = pltpu.make_async_copy(tabv, itab, sem_tab)
    to_scalars.start()

    phi = split(phi_ref[...])
    many_children = 4

    def along(i, _):
        rows = x_ref.shape[1]
        v = x_ref[pl.ds(i * many_children, many_children)].reshape(many_children * rows, 128)
        y = dot3(split(v), phi)
        for q in range(many_children):
            for half in range(2):
                hi, lo = split(y[q * rows : (q + 1) * rows, half * 128 : (half + 1) * 128])
                alh[i * many_children + q, half * rows : (half + 1) * rows, :] = hi
                all_[i * many_children + q, half * rows : (half + 1) * rows, :] = lo
        return 0

    def phases_on(c):
        for j in range(1, nd):
            zp_copy(c, j).wait_recv()
        for j in range(1, nb):
            pf_copy(c, j).start()
        pf[c, b] = zp[c]

    def shifts(c):
        for j in range(1, nb):
            pf_copy(c, j).wait_recv()
        def body(i, _):
            for d in range(nd):
                for j in range(own_tiles):
                    v = pf[c, i, d, j]
                    y = v * v
                    co, si = horner(y, COS), v * horner(y, SIN)
                    for p in range(2):
                        row = d * PER + 2 * (i * own_tiles + j) + p
                        flat[0, pl.ds(row, OCT, stride=R), :] = co
                        flat[1, pl.ds(row, OCT, stride=R), :] = si
            return 0

        lax.fori_loop(0, nb, body, 0)

        def place(o, _):
            rows = pl.ds(pl.multiple_of(o * R, 8), R)
            cc[c, o] = flat[0, rows, :]
            cs[c, o] = flat[1, rows, :]
            return 0

        lax.fori_loop(0, OCT, place, 0)

    def turn(c, o):
        return cc[c, o], cs[c, o]

    tf, tc = thetat_ref.shape
    tl = tc // nd

    def axis(shape, d):
        return lax.broadcasted_iota(I32, shape, d)

    def ones(shape, hit):
        return jnp.where(hit, 1.0, 0.0).astype(BF16)

    def fine_row(i):
        return (i >> 1) & (tf - 1)

    def polar_row(c, r):
        c, r = c + (r >> (R.bit_length() - 1)), r & (R - 1)
        return (r >> (PER.bit_length() - 1)) * tl + c * ROWS + ((r >> 2) & (ROWS - 1))

    def masks():
        shape = (PAIR * R, 4 * tf)
        r, k = axis(shape, 0), axis(shape, 1)
        hit = (((r >> 1) & 1) == jnp.where(k >= 2 * tf, 1, 0)) & ((r & 1) == (k & 1))
        mask[...] = ones(shape, hit)
        shape = (4 * tf, R)
        k, r = axis(shape, 0), axis(shape, 1)
        hit = (((r >> 1) & 1) == jnp.where(k >= 2 * tf, 1, 0)) & ((r & 1) == (k & 1))
        maskt[...] = ones(shape, hit)
        shape = (tf, 4 * tf)
        w = ones(shape, fine_row(axis(shape, 1)) == axis(shape, 0))
        shape = (4 * tf, tf)
        wt = ones(shape, fine_row(axis(shape, 0)) == axis(shape, 1))
        for v, out in zip(split(thetat_ref[...].T), (0, 1)):
            wide[out] = d32(v, w).astype(BF16)
        for v, out in zip(split(thetat_ref[...]), (0, 1)):
            widet[out] = d32(wt, v).astype(BF16)

    d32 = functools.partial(jnp.dot, preferred_element_type=F32)

    def spread_map(c):
        shape = (PAIR * R, tc)
        pick = ones(shape, polar_row(c, axis(shape, 0)) == axis(shape, 1))
        for i, out in enumerate((th, tl_)):
            out[...] = d32(pick, wide[i]).astype(BF16) * mask[...]

    def spread_map_back(c):
        shape = (tc, R)
        pick = ones(shape, polar_row(c, axis(shape, 1)) == axis(shape, 0))
        for i, source in enumerate((0, 0, 1)):
            tth[:, i * R : (i + 1) * R] = d32(widet[source], pick).astype(BF16) * maskt[...]

    gathered = set()

    def aggregate(c):
        c = c // PAIR * PAIR
        if c in gathered:
            return
        gathered.add(c)
        for e in range(PAIR):
            shifts(c + e)
        spread_map(c)

        def body(kk, sums):
            k = 2 * kk
            i0, i1 = itab[PERM, k], itab[PERM, k + 1]
            rh = jnp.concatenate([alh[i0], alh[i1]], axis=1)
            rl = jnp.concatenate([all_[i0], all_[i1]], axis=1)
            v = dot3((th[...], tl_[...]), (rh, rl))
            for q in range(2):
                o, keep = itab[OCTS, k + q], itab[KEEP, k + q].astype(F32)
                for e in range(PAIR):
                    w = v[e * R : (e + 1) * R, q * 128 : (q + 1) * 128]
                    for i, m in enumerate(turn(c + e, o)):
                        sums[2 * e + i] = sums[2 * e + i] * keep + m * w
                for e in range(2 * PAIR):
                    sb[k + q, e] = sums[e]
            return sums

        lax.fori_loop(0, n // 2, body, [jnp.zeros((R, 128), F32)] * (2 * PAIR))

        def pick(p, _):
            last, has = itab[LAST, p], itab[HAS, p].astype(F32)
            for e in range(PAIR):
                v, w = (sb[last, 2 * e + i].reshape(nd * GROUP, 8, 128) for i in range(2))
                below, above = neighbours(w)
                v = (v + jnp.where(even_rows(w.shape), -below, above)) * has
                part[c + e, :, :, p] = v.reshape(nd, GROUP, 8, 128)
            return 0

        lax.fori_loop(0, parents, pick, 0)

    def add(c, d, slot):
        def body(k, _):
            part[c, d, k] = part[c, d, k] + ar[c, slot, k]
            return 0

        lax.fori_loop(0, GROUP, body, 0)

    def send_end(c, j):
        @pl.when(z == 0)
        def _():
            right_copy(c, nd - 1 - j).start()

        @pl.when(z == nd - 1)
        def _():
            left_copy(c, j).start()

    def hop(c, t):
        d, k = nd - 1 + z - t, t - (nd - 1 - z)

        @pl.when(jnp.logical_and(z > 0, t >= z))
        def _():
            up_wait(c, d).wait_recv()
            add(c, d, d)
            right_copy(c, d).start()

        @pl.when(jnp.logical_and(z < nd - 1, k >= 0))
        def _():
            up_wait(c, k).wait_recv()
            add(c, k, k)
            left_copy(c, k).start()

    def finish_up(c):
        @pl.when(z > 0)
        def _():
            up_wait(c, z).wait_recv()
            add(c, z, z)

        @pl.when(z < nd - 1)
        def _():
            up_wait(c, nd).wait_recv()
            add(c, z, nd)

        for j in range(1, nb):
            q_copy(c, j).start()
        qa[c, b] = part[c, z, g]

    started = []

    def translate(c):
        if not started:
            started.append(c)
            for j in range(1, GROUP):
                far_copy(j).wait_recv()
            move = pltpu.make_async_copy(farr, fars, sem_fs)
            move.start()
            move.wait()
            for i in range(C):
                trans_copy(i).wait()
        for j in range(1, nb):
            q_copy(c, j).wait_recv()

        def stage(s, _):
            v = qa[c, s]
            below, above = neighbours(v)
            ql[pl.ds(s * parents, parents), 0] = v
            ql[pl.ds(s * parents, parents), 1] = jnp.where(even_rows(v.shape), below, above)
            return 0

        lax.fori_loop(0, nb, stage, 0)
        even = even_rows((8, 128))
        for jg in range(GROUP):

            def body(p, _):
                u = w = None
                for l in range(many):
                    f, kind = fars[jg, p, l], fars[jg, p, 64 + l]
                    a = trans[c, kind]
                    r, i = a * ql[f, 0], a * ql[f, 1]
                    u = r if u is None else u + r
                    w = i if w is None else w + i
                re = u - pltpu.roll(u, 7, 0)
                im = w + pltpu.roll(w, 1, 0)
                ts[c, jg, p] = jnp.where(even, re, im)
                return 0

            lax.fori_loop(0, parents, body, 0)
        for j in range(1, GROUP):
            t_copy(c, j).start()
        ta[c, g] = ts[c, g]

    def coarse_out(c):
        rows = pl.ds(c * PER, PER)
        return pltpu.make_async_copy(coarse_ref.at[:, rows], coarse_hbm.at[:, rows], sem_c.at[c])

    def coarse(c):
        for j in range(1, GROUP):
            t_copy(c, j).wait_recv()

        def body(p, _):
            rows = pl.ds(c * GROUP * 8, GROUP * 8)
            v = ta[c, :, p] + upper_ref[p, rows, :].reshape(GROUP, 8, 128)
            coarse_ref[p, rows, :] = v.reshape(GROUP * 8, 128)
            cg[c, z, :, p] = v
            return 0

        lax.fori_loop(0, parents, body, 0)
        coarse_out(c).start()

        @pl.when(z < nd - 1)
        def _():
            down_right(c, z).start()

        @pl.when(z > 0)
        def _():
            down_left(c, z).start()

    def pass_down(c, k):
        @pl.when(jnp.logical_and(z >= k, z < nd - 1))
        def _():
            down_right(c, z - k).wait_recv()
            down_right(c, z - k).start()

        @pl.when(jnp.logical_and(z + k < nd, z > 0))
        def _():
            down_left(c, z + k).wait_recv()
            down_left(c, z + k).start()

    spread = []

    def disaggregate(c):
        @pl.when(z == 0)
        def _():
            for d in range(1, nd):
                down_left(c, d).wait_recv()

        @pl.when(z == nd - 1)
        def _():
            for d in range(nd - 1):
                down_right(c, d).wait_recv()

        spread_map_back(c)

        def stage(p, _):
            v = cg[c, :, :, p].reshape(nd * GROUP, 8, 128)
            below, above = neighbours(v)
            xl[p] = v.reshape(R, 128)
            kl[p] = jnp.where(even_rows(v.shape), below, -above).reshape(R, 128)
            return 0

        lax.fori_loop(0, parents, stage, 0)
        spread.append(c)
        first, last = len(spread) == 1, len(spread) == C
        phi = split(phi_ref[...]) if last else None

        def pair(i):
            ys = []
            for q in range(2):
                p, o = itab[PARENT, i + q], itab[OCTANT, i + q]
                co, si = turn(c, o)
                ys.append(co * xl[p] + si * kl[p])
            hi, lo = split(jnp.concatenate(ys, axis=1))
            return d32(tth[...], jnp.concatenate([hi, lo, hi], axis=0))

        def body(ii, _):
            pairs = [pair(4 * ii), pair(4 * ii + 2)]
            for q in range(4):
                i = 4 * ii + q
                w = pairs[q // 2][:, q % 2 * 128 : (q % 2 + 1) * 128]
                if not first:
                    w = w + fa[i]
                if not last:
                    fa[i] = w
                else:
                    half = w.shape[0] // 2
                    line = jnp.concatenate([w[:half], w[half:]], axis=1)
                    fine_ref[i] = dot3(split(line), phi, turned=True)
            if last:
                done = pl.ds(4 * ii, 4)
                pltpu.make_async_copy(fine_ref.at[done], fine_hbm.at[done], sem_f).start()
            return 0

        lax.fori_loop(0, n // 4, body, 0)

    masks()
    for c in use:
        phases_on(c)
    x_in.wait()
    lax.fori_loop(0, n // many_children, along, 0)
    to_scalars.wait()
    upper_in.wait()

    def steps(c):
        yield functools.partial(aggregate, c)
        for j in range(nd - 1):
            yield functools.partial(send_end, c, j)
        for t in range(1, nd - 1):
            yield functools.partial(hop, c, t)
        yield functools.partial(finish_up, c)
        yield functools.partial(translate, c)
        yield functools.partial(coarse, c)
        for k in range(1, nd - 1):
            yield functools.partial(pass_down, c, k)
        yield functools.partial(disaggregate, c)

    each = [list(steps(c)) for c in range(C)]
    for c in order:
        each[c].pop(0)()
    assert not any(each)

    pltpu.make_async_copy(fine_ref, fine_hbm, sem_f).wait()
    for c in range(C):
        coarse_out(c).wait()

    for j in range(1, GROUP):
        far_copy(j).wait_send()

    def drain(c, _):
        for j in range(1, nd):
            zp_copy(c, j).wait_send()
        for j in range(1, nb):
            pf_copy(c, j).wait_send()
            q_copy(c, j).wait_send()
        for j in range(1, GROUP):
            t_copy(c, j).wait_send()
        for d in range(nd):

            @pl.when(d > z)
            def _():
                right_copy(c, d).wait_send()

            @pl.when(d < z)
            def _():
                left_copy(c, d).wait_send()

            @pl.when(jnp.logical_and(d <= z, z < nd - 1))
            def _():
                down_right(c, d).wait_send()

            @pl.when(jnp.logical_and(d >= z, z > 0))
            def _():
                down_left(c, d).wait_send()

        return 0

    lax.fori_loop(0, C, drain, 0)


def shards(
    fine_out,
    theta_interp,
    phi_interp,
    shift_phase,
    translation,
    upper_in,
    children,
    far_boxes,
    far_offsets,
):
    n = fine_out.shape[0]
    tc, tf = theta_interp.shape
    pf_, pc = phi_interp.shape
    parents, many = far_boxes.shape
    nb, nd = lax.axis_size("box"), lax.axis_size("dir")
    noff = translation.shape[0]
    tl = tc // nd
    ROWS = nb // FINE
    GROUP = ROWS // 2
    C = tl // ROWS
    R = nd * GROUP * 8
    PAIR = pair_of(R, C)

    phases = shift_phase.reshape(OCT, tl * 2, 128).transpose(1, 0, 2)

    vmem, smem, hbm = (
        pl.BlockSpec(memory_space=m) for m in (pltpu.VMEM, pltpu.SMEM, pl.ANY)
    )
    dma = pltpu.SemaphoreType.DMA
    tile = (GROUP, parents, 8, 128)
    rows, fine_rows = C * GROUP * 8, tf * 2
    coarse_in, fine_in = pl.pallas_call(
        functools.partial(kernel, (nb, nd, C, ROWS, n, parents, many)),
        in_specs=[smem] + [vmem] * 3 + [hbm] + [vmem] * 2 + [hbm] * 2,
        out_specs=[hbm, hbm],
        out_shape=[
            jax.ShapeDtypeStruct((parents, rows, 128), F32),
            jax.ShapeDtypeStruct((n, fine_rows, pf_), F32),
        ],
        scratch_shapes=[
            pltpu.VMEM((parents, rows, 128), F32),
            pltpu.VMEM((n, fine_rows, pf_), F32),
            pltpu.VMEM((n, fine_rows, pf_), F32),
            pltpu.VMEM((parents, rows, 128), F32),
            pltpu.VMEM((C, noff, 8, 128), F32),
            pltpu.VMEM((8, 128), I32),
            pltpu.SMEM((8, 128), I32),
            pltpu.VMEM((GROUP, parents, 128), I32),
            pltpu.SMEM((GROUP, parents, 128), I32),
            pltpu.VMEM((C, nd, 2 * ROWS // nb, OCT, 128), F32),
            pltpu.VMEM((C, nb, nd, 2 * ROWS // nb, OCT, 128), F32),
            pltpu.VMEM((C, OCT, R, 128), F32),
            pltpu.VMEM((C, OCT, R, 128), F32),
            pltpu.VMEM((2, OCT * R, 128), F32),
            pltpu.VMEM((n, 2 * fine_rows, 128), BF16),
            pltpu.VMEM((n, 2 * fine_rows, 128), BF16),
            pltpu.VMEM((PAIR * R, 4 * tf), BF16),
            pltpu.VMEM((PAIR * R, 4 * tf), BF16),
            pltpu.VMEM((4 * tf, 3 * R), BF16),
            pltpu.VMEM((2, tc, 4 * tf), BF16),
            pltpu.VMEM((2, 4 * tf, tc), BF16),
            pltpu.VMEM((PAIR * R, 4 * tf), BF16),
            pltpu.VMEM((4 * tf, R), BF16),
            pltpu.VMEM((n, 2 * PAIR, R, 128), F32),
            pltpu.VMEM((C, nd) + tile, F32),
            pltpu.VMEM((C, nd + 1) + tile, F32),
            pltpu.VMEM((C, nb) + tile[1:], F32),
            pltpu.VMEM((nb * parents, 2, 8, 128), F32),
            pltpu.VMEM((C,) + tile, F32),
            pltpu.VMEM((C,) + tile, F32),
            pltpu.VMEM((C, nd) + tile, F32),
            pltpu.VMEM((parents, R, 128), F32),
            pltpu.VMEM((parents, R, 128), F32),
            pltpu.VMEM((n, 4 * tf, 128), F32),
            dma,
            dma,
            dma((C,)),
            dma,
            dma((C,)),
            dma,
            dma,
            dma((GROUP,)),
            dma((GROUP,)),
            dma((C, nd)),
            dma((C, nd)),
            dma((C, nb)),
            dma((C, nb)),
            dma((C, nd)),
            dma((C, nd + 1)),
            dma((C, nb)),
            dma((C, nb)),
            dma((C, GROUP)),
            dma((C, GROUP)),
            dma((C, nd)),
            dma((C, nd)),
            dma((C, nd)),
        ],
        compiler_params=pltpu.CompilerParams(
            collective_id=0, has_side_effects=True, vmem_limit_bytes=VMEM_BYTES
        ),
    )(
        children.T,
        far_boxes,
        far_offsets,
        phases,
        rows_view(fine_out),
        phi_interp,
        theta_interp.T,
        rows_view(upper_in),
        rows_view(translation),
    )
    return rows_unview(coarse_in), rows_unview(fine_in)


def solution(mesh):
    placed = (
        P(("box", "dir"), None, None),
        P(),
        P(),
        P(None, "dir"),
        P(None, None, "dir"),
        P("box", None, "dir"),
        P("box", None),
        P("box", None),
        P("box", None),
    )
    return jax.shard_map(
        shards,
        mesh=mesh,
        in_specs=placed,
        out_specs=(P("box", None, "dir"), P(("box", "dir"), None, None)),
        check_vma=False,
    )
```

```python
import functools

import jax
import jax.numpy as jnp
from jax import lax
from jax.experimental import pallas as pl
from jax.experimental.pallas import tpu as pltpu
from jax.sharding import PartitionSpec as P

F32, BF16, I32 = jnp.float32, jnp.bfloat16, jnp.int32
MESH = pl.DeviceIdType.MESH
VMEM_BYTES = 60 * 1024 * 1024
FINE = 2
ORDERS = {
    (4, 8): (0, 1, 1, 0, 1, 1, 0, 2, 1, 0, 2, 0, 3, 3, 1, 5, 0, 2, 1, 3, 2, 3, 2, 4, 0, 3, 1, 5, 2, 3, 0, 2, 1, 3, 0, 5, 4, 5, 5, 4, 4, 6, 1, 0, 7, 2, 5, 4, 2, 0, 6, 7, 6, 7, 3, 5, 4, 6, 3, 0, 2, 4, 6, 7, 1, 5, 7, 2, 6, 4, 7, 5, 6, 4, 3, 7, 2, 5, 6, 3, 4, 7, 6, 3, 7, 4, 6, 1, 4, 6, 5, 7, 6, 5, 7, 7),
    (4, 4): (2, 2, 0, 0, 2, 0, 1, 2, 0, 1, 0, 2, 0, 2, 3, 0, 1, 3, 1, 1, 2, 0, 3, 1, 3, 2, 3, 0, 2, 1, 3, 1, 0, 1, 3, 2, 0, 3, 1, 2, 3, 1, 0, 2, 3, 1, 3, 3),
}
OCT = 8

COS = (
    0.999999999880854,
    -0.49999999845758136,
    0.04166666339221376,
    -0.001388886238622854,
    2.48005323812661e-05,
    -2.753445728365435e-07,
    2.0600835499376906e-09,
    -9.713911649043148e-12,
)
SIN = (
    0.9999999992304494,
    -0.166666659035747,
    0.008333320978968734,
    -0.00019840518737424315,
    2.7535517055355563e-06,
    -2.4725519533129986e-08,
    1.360099414116501e-10,
)


def split(x):
    hi = x.astype(BF16)
    return hi, (x - hi.astype(F32)).astype(BF16)


def dot3(a, b, turned=False):
    (ah, al), (bh, bl) = a, b
    sums = (((1,), (1 if turned else 0,)), ((), ()))
    d = functools.partial(lax.dot_general, dimension_numbers=sums, preferred_element_type=F32)
    return d(ah, bh) + (d(ah, bl) + d(al, bh))


def horner(y, coefficients):
    r = jnp.full_like(y, coefficients[-1])
    for c in coefficients[-2::-1]:
        r = r * y + c
    return r


def pair_of(rows, chunks):
    return 2 if rows <= 64 and chunks % 2 == 0 else 1


def rows_view(x):
    n, _, k = x.shape
    return x.reshape(n, 2, k // 128, 128).transpose(0, 2, 1, 3).reshape(n, k // 64, 128)


def rows_unview(x):
    n, r, _ = x.shape
    return x.reshape(n, r // 2, 2, 128).transpose(0, 2, 1, 3).reshape(n, 2, r * 64)


def neighbours(v):
    return pltpu.roll(v, 7, v.ndim - 2), pltpu.roll(v, 1, v.ndim - 2)


def even_rows(shape):
    return lax.broadcasted_iota(I32, shape, len(shape) - 2) % 2 == 0


def kernel(
    dims,
    children_ref,
    boxes_ref,
    kinds_ref,
    phase_ref,
    x_hbm,
    phi_ref,
    thetat_ref,
    upper_hbm,
    trans_ref,
    coarse_hbm,
    fine_hbm,
    coarse_ref,
    fine_ref,
    x_ref,
    upper_ref,
    trans,
    tabv,
    itab,
    farr,
    fars,
    zp,
    pf,
    cc,
    cs,
    flat,
    alh,
    all_,
    th,
    tl_,
    tth,
    wide,
    widet,
    mask,
    maskt,
    sb,
    part,
    ar,
    qa,
    ql,
    ts,
    ta,
    cg,
    xl,
    kl,
    fa,
    sem_x,
    sem_u,
    sem_c,
    sem_f,
    sem_tr,
    sem_fs,
    sem_tab,
    far_s,
    far_r,
    zp_s,
    zp_r,
    pf_s,
    pf_r,
    up_s,
    up_r,
    q_s,
    q_r,
    t_s,
    t_r,
    dr_s,
    dl_s,
    d_r,
):
    nb, nd, C, ROWS, n, parents, many = dims
    GROUP = ROWS // 2
    PER = GROUP * 8
    R = nd * PER
    PAIR = pair_of(R, C)
    b, z = lax.axis_index("box"), lax.axis_index("dir")
    g, h = b % GROUP, b // GROUP
    own_tiles = 2 * ROWS // nb
    count = 3 * nd
    order = ORDERS.get((nd, C)) or [
        c for _, c in sorted((c * (count // 2) + i, c) for c in range(C) for i in range(count))
    ]
    PERM, OCTS, PARENT, OCTANT, LAST, KEEP, HAS = range(7)

    def remote(src, dst, ss, rs, dev):
        return pltpu.make_async_remote_copy(
            src_ref=src, dst_ref=dst, send_sem=ss, recv_sem=rs, device_id=dev, device_id_type=MESH
        )

    def zp_copy(c, j):
        to = (z + j) % nd
        return remote(
            phase_ref.at[pl.ds(c * 2 * ROWS + b * own_tiles, own_tiles)],
            zp.at[c, z],
            zp_s.at[c, j],
            zp_r.at[c, j],
            (b, to),
        )

    def pf_copy(c, j):
        return remote(zp.at[c], pf.at[c, b], pf_s.at[c, j], pf_r.at[c, j], (b ^ j, z))

    def far_copy(j):
        return remote(farr.at[g], farr.at[g], far_s.at[j], far_r.at[j], (b ^ j, z))

    def right_copy(c, d):
        return remote(part.at[c, d], ar.at[c, d], up_s.at[c, d], up_r.at[c, d], (b, z + 1))

    def left_copy(c, d):
        slot = jnp.where(z - 1 == d, nd, d)
        return remote(part.at[c, d], ar.at[c, slot], up_s.at[c, d], up_r.at[c, slot], (b, z - 1))

    def up_wait(c, slot):
        return remote(part.at[c, 0], ar.at[c, slot], up_s.at[c, 0], up_r.at[c, slot], (b, z))

    def q_copy(c, j):
        to = b ^ j
        return remote(
            part.at[c, z, to % GROUP], qa.at[c, b], q_s.at[c, j], q_r.at[c, j], (to, z)
        )

    def t_copy(c, j):
        return remote(ts.at[c, g ^ j], ta.at[c, g], t_s.at[c, j], t_r.at[c, j], (b ^ j, z))

    def down_right(c, d):
        return remote(cg.at[c, d], cg.at[c, d], dr_s.at[c, d], d_r.at[c, d], (b, z + 1))

    def down_left(c, d):
        return remote(cg.at[c, d], cg.at[c, d], dl_s.at[c, d], d_r.at[c, d], (b, z - 1))

    def trans_copy(c):
        row = pl.multiple_of((c * GROUP + g) * 8, 8)
        return pltpu.make_async_copy(trans_ref.at[:, pl.ds(row, 8)], trans.at[c], sem_tr.at[c])

    x_in = pltpu.make_async_copy(x_hbm, x_ref, sem_x)
    upper_in = pltpu.make_async_copy(upper_hbm, upper_ref, sem_u)
    x_in.start()
    upper_in.start()
    for c in range(C):
        trans_copy(c).start()

    farr[g, :, 0:many] = boxes_ref[...]
    farr[g, :, 64 : 64 + many] = kinds_ref[...]
    barrier = pltpu.get_barrier_semaphore()
    for j in range(1, nb):
        pl.semaphore_signal(barrier, inc=1, device_id=(b ^ j, z), device_id_type=MESH)
    for j in range(1, nd):
        pl.semaphore_signal(barrier, inc=1, device_id=(b, (z + j) % nd), device_id_type=MESH)
    pl.semaphore_wait(barrier, nb + nd - 2)

    use = [q for p in dict.fromkeys(c // PAIR for c in order) for q in range(p * PAIR, (p + 1) * PAIR)]
    for c in use:
        for j in range(1, nd):
            zp_copy(c, j).start()
    for j in range(1, GROUP):
        far_copy(j).start()
    for c in range(C):
        zp[c, z] = phase_ref[pl.ds(c * 2 * ROWS + b * own_tiles, own_tiles)]

    lanes = lax.broadcasted_iota(I32, (1, 128), 1)

    def table(p, carry):
        k, rows = carry[0], list(carry[1:])
        first = k
        for o in range(OCT):
            local = lax.rem(children_ref[o, p], n * nd) - z * n
            own = jnp.logical_and(local >= 0, local < n)
            here, at = lanes == jnp.where(own, k, -1), lanes == jnp.where(own, local, -1)
            rows[PERM] = jnp.where(here, local, rows[PERM])
            rows[OCTS] = jnp.where(here, o, rows[OCTS])
            rows[KEEP] = jnp.where(here, jnp.where(k > first, 1, 0), rows[KEEP])
            rows[PARENT] = jnp.where(at, p, rows[PARENT])
            rows[OCTANT] = jnp.where(at, o, rows[OCTANT])
            k = k + jnp.where(own, 1, 0)
        rows[LAST] = jnp.where(lanes == p, jnp.clip(k - 1, 0, n - 1), rows[LAST])
        rows[HAS] = jnp.where(lanes == p, jnp.where(k > first, 1, 0), rows[HAS])
        return (k, *rows)

    none = jnp.zeros((1, 128), I32)
    found = lax.fori_loop(0, parents, table, (jnp.int32(0), *[none] * 7))
    for i in range(7):
        tabv[i : i + 1, :] = found[1 + i]
    tabv[7:8, :] = none
    to_scalars = pltpu.make_async_copy(tabv, itab, sem_tab)
    to_scalars.start()

    phi = split(phi_ref[...])
    many_children = 4

    def along(i, _):
        rows = x_ref.shape[1]
        v = x_ref[pl.ds(i * many_children, many_children)].reshape(many_children * rows, 128)
        y = dot3(split(v), phi)
        for q in range(many_children):
            for half in range(2):
                hi, lo = split(y[q * rows : (q + 1) * rows, half * 128 : (half + 1) * 128])
                alh[i * many_children + q, half * rows : (half + 1) * rows, :] = hi
                all_[i * many_children + q, half * rows : (half + 1) * rows, :] = lo
        return 0

    def phases_on(c):
        for j in range(1, nd):
            zp_copy(c, j).wait_recv()
        for j in range(1, nb):
            pf_copy(c, j).start()
        pf[c, b] = zp[c]

    def shifts(c):
        for j in range(1, nb):
            pf_copy(c, j).wait_recv()
        def body(i, _):
            for d in range(nd):
                for j in range(own_tiles):
                    v = pf[c, i, d, j]
                    y = v * v
                    co, si = horner(y, COS), v * horner(y, SIN)
                    for p in range(2):
                        row = d * PER + 2 * (i * own_tiles + j) + p
                        flat[0, pl.ds(row, OCT, stride=R), :] = co
                        flat[1, pl.ds(row, OCT, stride=R), :] = si
            return 0

        lax.fori_loop(0, nb, body, 0)

        def place(o, _):
            rows = pl.ds(pl.multiple_of(o * R, 8), R)
            cc[c, o] = flat[0, rows, :]
            cs[c, o] = flat[1, rows, :]
            return 0

        lax.fori_loop(0, OCT, place, 0)

    def turn(c, o):
        return cc[c, o], cs[c, o]

    tf, tc = thetat_ref.shape
    tl = tc // nd

    def axis(shape, d):
        return lax.broadcasted_iota(I32, shape, d)

    def ones(shape, hit):
        return jnp.where(hit, 1.0, 0.0).astype(BF16)

    def fine_row(i):
        return (i >> 1) & (tf - 1)

    def polar_row(c, r):
        c, r = c + (r >> (R.bit_length() - 1)), r & (R - 1)
        return (r >> (PER.bit_length() - 1)) * tl + c * ROWS + ((r >> 2) & (ROWS - 1))

    def masks():
        shape = (PAIR * R, 4 * tf)
        r, k = axis(shape, 0), axis(shape, 1)
        hit = (((r >> 1) & 1) == jnp.where(k >= 2 * tf, 1, 0)) & ((r & 1) == (k & 1))
        mask[...] = ones(shape, hit)
        shape = (4 * tf, R)
        k, r = axis(shape, 0), axis(shape, 1)
        hit = (((r >> 1) & 1) == jnp.where(k >= 2 * tf, 1, 0)) & ((r & 1) == (k & 1))
        maskt[...] = ones(shape, hit)
        shape = (tf, 4 * tf)
        w = ones(shape, fine_row(axis(shape, 1)) == axis(shape, 0))
        shape = (4 * tf, tf)
        wt = ones(shape, fine_row(axis(shape, 0)) == axis(shape, 1))
        for v, out in zip(split(thetat_ref[...].T), (0, 1)):
            wide[out] = d32(v, w).astype(BF16)
        for v, out in zip(split(thetat_ref[...]), (0, 1)):
            widet[out] = d32(wt, v).astype(BF16)

    d32 = functools.partial(jnp.dot, preferred_element_type=F32)

    def spread_map(c):
        shape = (PAIR * R, tc)
        pick = ones(shape, polar_row(c, axis(shape, 0)) == axis(shape, 1))
        for i, out in enumerate((th, tl_)):
            out[...] = d32(pick, wide[i]).astype(BF16) * mask[...]

    def spread_map_back(c):
        shape = (tc, R)
        pick = ones(shape, polar_row(c, axis(shape, 1)) == axis(shape, 0))
        for i, source in enumerate((0, 0, 1)):
            tth[:, i * R : (i + 1) * R] = d32(widet[source], pick).astype(BF16) * maskt[...]

    gathered = set()

    def aggregate(c):
        c = c // PAIR * PAIR
        if c in gathered:
            return
        gathered.add(c)
        for e in range(PAIR):
            shifts(c + e)
        spread_map(c)

        def body(kk, sums):
            k = 2 * kk
            i0, i1 = itab[PERM, k], itab[PERM, k + 1]
            rh = jnp.concatenate([alh[i0], alh[i1]], axis=1)
            rl = jnp.concatenate([all_[i0], all_[i1]], axis=1)
            v = dot3((th[...], tl_[...]), (rh, rl))
            for q in range(2):
                o, keep = itab[OCTS, k + q], itab[KEEP, k + q].astype(F32)
                for e in range(PAIR):
                    w = v[e * R : (e + 1) * R, q * 128 : (q + 1) * 128]
                    for i, m in enumerate(turn(c + e, o)):
                        sums[2 * e + i] = sums[2 * e + i] * keep + m * w
                for e in range(2 * PAIR):
                    sb[k + q, e] = sums[e]
            return sums

        lax.fori_loop(0, n // 2, body, [jnp.zeros((R, 128), F32)] * (2 * PAIR))

        def pick(p, _):
            last, has = itab[LAST, p], itab[HAS, p].astype(F32)
            for e in range(PAIR):
                v, w = (sb[last, 2 * e + i].reshape(nd * GROUP, 8, 128) for i in range(2))
                below, above = neighbours(w)
                v = (v + jnp.where(even_rows(w.shape), -below, above)) * has
                part[c + e, :, :, p] = v.reshape(nd, GROUP, 8, 128)
            return 0

        lax.fori_loop(0, parents, pick, 0)

    def add(c, d, slot):
        def body(k, _):
            part[c, d, k] = part[c, d, k] + ar[c, slot, k]
            return 0

        lax.fori_loop(0, GROUP, body, 0)

    def send_end(c, j):
        @pl.when(z == 0)
        def _():
            right_copy(c, nd - 1 - j).start()

        @pl.when(z == nd - 1)
        def _():
            left_copy(c, j).start()

    def hop(c, t):
        d, k = nd - 1 + z - t, t - (nd - 1 - z)

        @pl.when(jnp.logical_and(z > 0, t >= z))
        def _():
            up_wait(c, d).wait_recv()
            add(c, d, d)
            right_copy(c, d).start()

        @pl.when(jnp.logical_and(z < nd - 1, k >= 0))
        def _():
            up_wait(c, k).wait_recv()
            add(c, k, k)
            left_copy(c, k).start()

    def finish_up(c):
        @pl.when(z > 0)
        def _():
            up_wait(c, z).wait_recv()
            add(c, z, z)

        @pl.when(z < nd - 1)
        def _():
            up_wait(c, nd).wait_recv()
            add(c, z, nd)

        for j in range(1, nb):
            q_copy(c, j).start()
        qa[c, b] = part[c, z, g]

    started = []

    def translate(c):
        if not started:
            started.append(c)
            for j in range(1, GROUP):
                far_copy(j).wait_recv()
            move = pltpu.make_async_copy(farr, fars, sem_fs)
            move.start()
            move.wait()
            for i in range(C):
                trans_copy(i).wait()
        for j in range(1, nb):
            q_copy(c, j).wait_recv()

        def stage(s, _):
            v = qa[c, s]
            below, above = neighbours(v)
            ql[pl.ds(s * parents, parents), 0] = v
            ql[pl.ds(s * parents, parents), 1] = jnp.where(even_rows(v.shape), below, above)
            return 0

        lax.fori_loop(0, nb, stage, 0)
        even = even_rows((8, 128))
        for jg in range(GROUP):

            def body(p, _):
                u = w = None
                for l in range(many):
                    f, kind = fars[jg, p, l], fars[jg, p, 64 + l]
                    a = trans[c, kind]
                    r, i = a * ql[f, 0], a * ql[f, 1]
                    u = r if u is None else u + r
                    w = i if w is None else w + i
                re = u - pltpu.roll(u, 7, 0)
                im = w + pltpu.roll(w, 1, 0)
                ts[c, jg, p] = jnp.where(even, re, im)
                return 0

            lax.fori_loop(0, parents, body, 0)
        for j in range(1, GROUP):
            t_copy(c, j).start()
        ta[c, g] = ts[c, g]

    def coarse_out(c):
        rows = pl.ds(c * PER, PER)
        return pltpu.make_async_copy(coarse_ref.at[:, rows], coarse_hbm.at[:, rows], sem_c.at[c])

    def coarse(c):
        for j in range(1, GROUP):
            t_copy(c, j).wait_recv()

        def body(p, _):
            rows = pl.ds(c * GROUP * 8, GROUP * 8)
            v = ta[c, :, p] + upper_ref[p, rows, :].reshape(GROUP, 8, 128)
            coarse_ref[p, rows, :] = v.reshape(GROUP * 8, 128)
            cg[c, z, :, p] = v
            return 0

        lax.fori_loop(0, parents, body, 0)
        coarse_out(c).start()

        @pl.when(z < nd - 1)
        def _():
            down_right(c, z).start()

        @pl.when(z > 0)
        def _():
            down_left(c, z).start()

    def pass_down(c, k):
        @pl.when(jnp.logical_and(z >= k, z < nd - 1))
        def _():
            down_right(c, z - k).wait_recv()
            down_right(c, z - k).start()

        @pl.when(jnp.logical_and(z + k < nd, z > 0))
        def _():
            down_left(c, z + k).wait_recv()
            down_left(c, z + k).start()

    spread = []

    def disaggregate(c):
        @pl.when(z == 0)
        def _():
            for d in range(1, nd):
                down_left(c, d).wait_recv()

        @pl.when(z == nd - 1)
        def _():
            for d in range(nd - 1):
                down_right(c, d).wait_recv()

        spread_map_back(c)

        def stage(p, _):
            v = cg[c, :, :, p].reshape(nd * GROUP, 8, 128)
            below, above = neighbours(v)
            xl[p] = v.reshape(R, 128)
            kl[p] = jnp.where(even_rows(v.shape), below, -above).reshape(R, 128)
            return 0

        lax.fori_loop(0, parents, stage, 0)
        spread.append(c)
        first, last = len(spread) == 1, len(spread) == C
        phi = split(phi_ref[...]) if last else None

        def pair(i):
            ys = []
            for q in range(2):
                p, o = itab[PARENT, i + q], itab[OCTANT, i + q]
                co, si = turn(c, o)
                ys.append(co * xl[p] + si * kl[p])
            hi, lo = split(jnp.concatenate(ys, axis=1))
            return d32(tth[...], jnp.concatenate([hi, lo, hi], axis=0))

        def body(ii, _):
            pairs = [pair(4 * ii), pair(4 * ii + 2)]
            for q in range(4):
                i = 4 * ii + q
                w = pairs[q // 2][:, q % 2 * 128 : (q % 2 + 1) * 128]
                if not first:
                    w = w + fa[i]
                if not last:
                    fa[i] = w
                else:
                    half = w.shape[0] // 2
                    line = jnp.concatenate([w[:half], w[half:]], axis=1)
                    fine_ref[i] = dot3(split(line), phi, turned=True)
            if last:
                done = pl.ds(4 * ii, 4)
                pltpu.make_async_copy(fine_ref.at[done], fine_hbm.at[done], sem_f).start()
            return 0

        lax.fori_loop(0, n // 4, body, 0)

    masks()
    for c in use:
        phases_on(c)
    x_in.wait()
    lax.fori_loop(0, n // many_children, along, 0)
    to_scalars.wait()
    upper_in.wait()

    def steps(c):
        yield functools.partial(aggregate, c)
        for j in range(nd - 1):
            yield functools.partial(send_end, c, j)
        for t in range(1, nd - 1):
            yield functools.partial(hop, c, t)
        yield functools.partial(finish_up, c)
        yield functools.partial(translate, c)
        yield functools.partial(coarse, c)
        for k in range(1, nd - 1):
            yield functools.partial(pass_down, c, k)
        yield functools.partial(disaggregate, c)

    each = [list(steps(c)) for c in range(C)]
    for c in order:
        each[c].pop(0)()
    assert not any(each)

    pltpu.make_async_copy(fine_ref, fine_hbm, sem_f).wait()
    for c in range(C):
        coarse_out(c).wait()

    for j in range(1, GROUP):
        far_copy(j).wait_send()

    def drain(c, _):
        for j in range(1, nd):
            zp_copy(c, j).wait_send()
        for j in range(1, nb):
            pf_copy(c, j).wait_send()
            q_copy(c, j).wait_send()
        for j in range(1, GROUP):
            t_copy(c, j).wait_send()
        for d in range(nd):

            @pl.when(d > z)
            def _():
                right_copy(c, d).wait_send()

            @pl.when(d < z)
            def _():
                left_copy(c, d).wait_send()

            @pl.when(jnp.logical_and(d <= z, z < nd - 1))
            def _():
                down_right(c, d).wait_send()

            @pl.when(jnp.logical_and(d >= z, z > 0))
            def _():
                down_left(c, d).wait_send()

        return 0

    lax.fori_loop(0, C, drain, 0)


def shards(
    fine_out,
    theta_interp,
    phi_interp,
    shift_phase,
    translation,
    upper_in,
    children,
    far_boxes,
    far_offsets,
):
    n = fine_out.shape[0]
    tc, tf = theta_interp.shape
    pf_, pc = phi_interp.shape
    parents, many = far_boxes.shape
    nb, nd = lax.axis_size("box"), lax.axis_size("dir")
    noff = translation.shape[0]
    tl = tc // nd
    ROWS = nb // FINE
    GROUP = ROWS // 2
    C = tl // ROWS
    R = nd * GROUP * 8
    PAIR = pair_of(R, C)

    phases = shift_phase.reshape(OCT, tl * 2, 128).transpose(1, 0, 2)

    vmem, smem, hbm = (
        pl.BlockSpec(memory_space=m) for m in (pltpu.VMEM, pltpu.SMEM, pl.ANY)
    )
    dma = pltpu.SemaphoreType.DMA
    tile = (GROUP, parents, 8, 128)
    rows, fine_rows = C * GROUP * 8, tf * 2
    coarse_in, fine_in = pl.pallas_call(
        functools.partial(kernel, (nb, nd, C, ROWS, n, parents, many)),
        in_specs=[smem] + [vmem] * 3 + [hbm] + [vmem] * 2 + [hbm] * 2,
        out_specs=[hbm, hbm],
        out_shape=[
            jax.ShapeDtypeStruct((parents, rows, 128), F32),
            jax.ShapeDtypeStruct((n, fine_rows, pf_), F32),
        ],
        scratch_shapes=[
            pltpu.VMEM((parents, rows, 128), F32),
            pltpu.VMEM((n, fine_rows, pf_), F32),
            pltpu.VMEM((n, fine_rows, pf_), F32),
            pltpu.VMEM((parents, rows, 128), F32),
            pltpu.VMEM((C, noff, 8, 128), F32),
            pltpu.VMEM((8, 128), I32),
            pltpu.SMEM((8, 128), I32),
            pltpu.VMEM((GROUP, parents, 128), I32),
            pltpu.SMEM((GROUP, parents, 128), I32),
            pltpu.VMEM((C, nd, 2 * ROWS // nb, OCT, 128), F32),
            pltpu.VMEM((C, nb, nd, 2 * ROWS // nb, OCT, 128), F32),
            pltpu.VMEM((C, OCT, R, 128), F32),
            pltpu.VMEM((C, OCT, R, 128), F32),
            pltpu.VMEM((2, OCT * R, 128), F32),
            pltpu.VMEM((n, 2 * fine_rows, 128), BF16),
            pltpu.VMEM((n, 2 * fine_rows, 128), BF16),
            pltpu.VMEM((PAIR * R, 4 * tf), BF16),
            pltpu.VMEM((PAIR * R, 4 * tf), BF16),
            pltpu.VMEM((4 * tf, 3 * R), BF16),
            pltpu.VMEM((2, tc, 4 * tf), BF16),
            pltpu.VMEM((2, 4 * tf, tc), BF16),
            pltpu.VMEM((PAIR * R, 4 * tf), BF16),
            pltpu.VMEM((4 * tf, R), BF16),
            pltpu.VMEM((n, 2 * PAIR, R, 128), F32),
            pltpu.VMEM((C, nd) + tile, F32),
            pltpu.VMEM((C, nd + 1) + tile, F32),
            pltpu.VMEM((C, nb) + tile[1:], F32),
            pltpu.VMEM((nb * parents, 2, 8, 128), F32),
            pltpu.VMEM((C,) + tile, F32),
            pltpu.VMEM((C,) + tile, F32),
            pltpu.VMEM((C, nd) + tile, F32),
            pltpu.VMEM((parents, R, 128), F32),
            pltpu.VMEM((parents, R, 128), F32),
            pltpu.VMEM((n, 4 * tf, 128), F32),
            dma,
            dma,
            dma((C,)),
            dma,
            dma((C,)),
            dma,
            dma,
            dma((GROUP,)),
            dma((GROUP,)),
            dma((C, nd)),
            dma((C, nd)),
            dma((C, nb)),
            dma((C, nb)),
            dma((C, nd)),
            dma((C, nd + 1)),
            dma((C, nb)),
            dma((C, nb)),
            dma((C, GROUP)),
            dma((C, GROUP)),
            dma((C, nd)),
            dma((C, nd)),
            dma((C, nd)),
        ],
        compiler_params=pltpu.CompilerParams(
            collective_id=0, has_side_effects=True, vmem_limit_bytes=VMEM_BYTES
        ),
    )(
        children.T,
        far_boxes,
        far_offsets,
        phases,
        rows_view(fine_out),
        phi_interp,
        theta_interp.T,
        rows_view(upper_in),
        rows_view(translation),
    )
    return rows_unview(coarse_in), rows_unview(fine_in)


def solution(mesh):
    placed = (
        P(("box", "dir"), None, None),
        P(),
        P(),
        P(None, "dir"),
        P(None, None, "dir"),
        P("box", None, "dir"),
        P("box", None),
        P("box", None),
        P("box", None),
    )
    return jax.shard_map(
        shards,
        mesh=mesh,
        in_specs=placed,
        out_specs=(P("box", None, "dir"), P(("box", "dir"), None, None)),
        check_vma=False,
    )
```

```python
import functools

import jax
import jax.numpy as jnp
from jax import lax
from jax.experimental import pallas as pl
from jax.experimental.pallas import tpu as pltpu
from jax.sharding import PartitionSpec as P

F32, BF16, I32 = jnp.float32, jnp.bfloat16, jnp.int32
MESH = pl.DeviceIdType.MESH
VMEM_BYTES = 60 * 1024 * 1024
FINE = 2
ORDERS = {
    (4, 8): (0, 1, 1, 0, 1, 1, 0, 2, 1, 0, 2, 0, 3, 3, 1, 5, 0, 2, 1, 3, 2, 3, 2, 4, 0, 3, 1, 5, 2, 3, 0, 2, 1, 3, 0, 5, 4, 5, 5, 4, 4, 6, 1, 0, 7, 2, 5, 4, 2, 0, 6, 7, 6, 7, 3, 5, 4, 6, 3, 0, 2, 4, 6, 7, 1, 5, 7, 2, 6, 4, 7, 5, 6, 4, 3, 7, 2, 5, 6, 3, 4, 7, 6, 3, 7, 4, 6, 1, 4, 6, 5, 7, 6, 5, 7, 7),
    (4, 4): (2, 2, 0, 0, 2, 0, 1, 2, 0, 1, 0, 2, 0, 2, 3, 0, 1, 3, 1, 1, 2, 0, 3, 1, 3, 2, 3, 0, 2, 1, 3, 1, 0, 1, 3, 2, 0, 3, 1, 2, 3, 1, 0, 2, 3, 1, 3, 3),
}
OCT = 8

COS = (
    0.999999999880854,
    -0.49999999845758136,
    0.04166666339221376,
    -0.001388886238622854,
    2.48005323812661e-05,
    -2.753445728365435e-07,
    2.0600835499376906e-09,
    -9.713911649043148e-12,
)
SIN = (
    0.9999999992304494,
    -0.166666659035747,
    0.008333320978968734,
    -0.00019840518737424315,
    2.7535517055355563e-06,
    -2.4725519533129986e-08,
    1.360099414116501e-10,
)


def split(x):
    hi = x.astype(BF16)
    return hi, (x - hi.astype(F32)).astype(BF16)


def dot3(a, b, turned=False):
    (ah, al), (bh, bl) = a, b
    sums = (((1,), (1 if turned else 0,)), ((), ()))
    d = functools.partial(lax.dot_general, dimension_numbers=sums, preferred_element_type=F32)
    return d(ah, bh) + (d(ah, bl) + d(al, bh))


def horner(y, coefficients):
    r = jnp.full_like(y, coefficients[-1])
    for c in coefficients[-2::-1]:
        r = r * y + c
    return r


def pair_of(rows, chunks):
    return 2 if rows <= 64 and chunks % 2 == 0 else 1


def rows_view(x):
    n, _, k = x.shape
    return x.reshape(n, 2, k // 128, 128).transpose(0, 2, 1, 3).reshape(n, k // 64, 128)


def rows_unview(x):
    n, r, _ = x.shape
    return x.reshape(n, r // 2, 2, 128).transpose(0, 2, 1, 3).reshape(n, 2, r * 64)


def neighbours(v):
    return pltpu.roll(v, 7, v.ndim - 2), pltpu.roll(v, 1, v.ndim - 2)


def even_rows(shape):
    return lax.broadcasted_iota(I32, shape, len(shape) - 2) % 2 == 0


def kernel(
    dims,
    children_ref,
    boxes_ref,
    kinds_ref,
    phase_ref,
    x_hbm,
    phi_ref,
    thetat_ref,
    upper_hbm,
    trans_ref,
    coarse_hbm,
    fine_hbm,
    coarse_ref,
    fine_ref,
    x_ref,
    upper_ref,
    trans,
    tabv,
    itab,
    farr,
    fars,
    zp,
    pf,
    cc,
    cs,
    flat,
    alh,
    all_,
    th,
    tl_,
    tth,
    wide,
    widet,
    mask,
    maskt,
    sb,
    part,
    ar,
    qa,
    ql,
    ts,
    ta,
    cg,
    xl,
    kl,
    fa,
    sem_x,
    sem_u,
    sem_c,
    sem_f,
    sem_tr,
    sem_fs,
    sem_tab,
    far_s,
    far_r,
    zp_s,
    zp_r,
    pf_s,
    pf_r,
    up_s,
    up_r,
    q_s,
    q_r,
    t_s,
    t_r,
    dr_s,
    dl_s,
    d_r,
):
    nb, nd, C, ROWS, n, parents, many = dims
    GROUP = ROWS // 2
    PER = GROUP * 8
    R = nd * PER
    PAIR = pair_of(R, C)
    b, z = lax.axis_index("box"), lax.axis_index("dir")
    g, h = b % GROUP, b // GROUP
    own_tiles = 2 * ROWS // nb
    count = 3 * nd
    order = ORDERS.get((nd, C)) or [
        c for _, c in sorted((c * (count // 2) + i, c) for c in range(C) for i in range(count))
    ]
    PERM, OCTS, PARENT, OCTANT, LAST, KEEP, HAS = range(7)

    def remote(src, dst, ss, rs, dev):
        return pltpu.make_async_remote_copy(
            src_ref=src, dst_ref=dst, send_sem=ss, recv_sem=rs, device_id=dev, device_id_type=MESH
        )

    def zp_copy(c, j):
        to = (z + j) % nd
        return remote(
            phase_ref.at[pl.ds(c * 2 * ROWS + b * own_tiles, own_tiles)],
            zp.at[c, z],
            zp_s.at[c, j],
            zp_r.at[c, j],
            (b, to),
        )

    def pf_copy(c, j):
        return remote(zp.at[c], pf.at[c, b], pf_s.at[c, j], pf_r.at[c, j], (b ^ j, z))

    def far_copy(j):
        return remote(farr.at[g], farr.at[g], far_s.at[j], far_r.at[j], (b ^ j, z))

    def right_copy(c, d):
        return remote(part.at[c, d], ar.at[c, d], up_s.at[c, d], up_r.at[c, d], (b, z + 1))

    def left_copy(c, d):
        slot = jnp.where(z - 1 == d, nd, d)
        return remote(part.at[c, d], ar.at[c, slot], up_s.at[c, d], up_r.at[c, slot], (b, z - 1))

    def up_wait(c, slot):
        return remote(part.at[c, 0], ar.at[c, slot], up_s.at[c, 0], up_r.at[c, slot], (b, z))

    def q_copy(c, j):
        to = b ^ j
        return remote(
            part.at[c, z, to % GROUP], qa.at[c, b], q_s.at[c, j], q_r.at[c, j], (to, z)
        )

    def t_copy(c, j):
        return remote(ts.at[c, g ^ j], ta.at[c, g], t_s.at[c, j], t_r.at[c, j], (b ^ j, z))

    def down_right(c, d):
        return remote(cg.at[c, d], cg.at[c, d], dr_s.at[c, d], d_r.at[c, d], (b, z + 1))

    def down_left(c, d):
        return remote(cg.at[c, d], cg.at[c, d], dl_s.at[c, d], d_r.at[c, d], (b, z - 1))

    def trans_copy(c):
        row = pl.multiple_of((c * GROUP + g) * 8, 8)
        return pltpu.make_async_copy(trans_ref.at[:, pl.ds(row, 8)], trans.at[c], sem_tr.at[c])

    x_in = pltpu.make_async_copy(x_hbm, x_ref, sem_x)
    upper_in = pltpu.make_async_copy(upper_hbm, upper_ref, sem_u)
    x_in.start()
    upper_in.start()
    for c in range(C):
        trans_copy(c).start()

    farr[g, :, 0:many] = boxes_ref[...]
    farr[g, :, 64 : 64 + many] = kinds_ref[...]
    barrier = pltpu.get_barrier_semaphore()
    for j in range(1, nb):
        pl.semaphore_signal(barrier, inc=1, device_id=(b ^ j, z), device_id_type=MESH)
    for j in range(1, nd):
        pl.semaphore_signal(barrier, inc=1, device_id=(b, (z + j) % nd), device_id_type=MESH)
    pl.semaphore_wait(barrier, nb + nd - 2)

    use = [q for p in dict.fromkeys(c // PAIR for c in order) for q in range(p * PAIR, (p + 1) * PAIR)]
    for c in use:
        for j in range(1, nd):
            zp_copy(c, j).start()
    for j in range(1, GROUP):
        far_copy(j).start()
    for c in range(C):
        zp[c, z] = phase_ref[pl.ds(c * 2 * ROWS + b * own_tiles, own_tiles)]

    lanes = lax.broadcasted_iota(I32, (1, 128), 1)

    def table(p, carry):
        k, rows = carry[0], list(carry[1:])
        first = k
        for o in range(OCT):
            local = lax.rem(children_ref[o, p], n * nd) - z * n
            own = jnp.logical_and(local >= 0, local < n)
            here, at = lanes == jnp.where(own, k, -1), lanes == jnp.where(own, local, -1)
            rows[PERM] = jnp.where(here, local, rows[PERM])
            rows[OCTS] = jnp.where(here, o, rows[OCTS])
            rows[KEEP] = jnp.where(here, jnp.where(k > first, 1, 0), rows[KEEP])
            rows[PARENT] = jnp.where(at, p, rows[PARENT])
            rows[OCTANT] = jnp.where(at, o, rows[OCTANT])
            k = k + jnp.where(own, 1, 0)
        rows[LAST] = jnp.where(lanes == p, jnp.clip(k - 1, 0, n - 1), rows[LAST])
        rows[HAS] = jnp.where(lanes == p, jnp.where(k > first, 1, 0), rows[HAS])
        return (k, *rows)

    none = jnp.zeros((1, 128), I32)
    found = lax.fori_loop(0, parents, table, (jnp.int32(0), *[none] * 7))
    for i in range(7):
        tabv[i : i + 1, :] = found[1 + i]
    tabv[7:8, :] = none
    to_scalars = pltpu.make_async_copy(tabv, itab, sem_tab)
    to_scalars.start()

    phi = split(phi_ref[...])
    many_children = 4

    def along(i, _):
        rows = x_ref.shape[1]
        v = x_ref[pl.ds(i * many_children, many_children)].reshape(many_children * rows, 128)
        y = dot3(split(v), phi)
        for q in range(many_children):
            for half in range(2):
                hi, lo = split(y[q * rows : (q + 1) * rows, half * 128 : (half + 1) * 128])
                alh[i * many_children + q, half * rows : (half + 1) * rows, :] = hi
                all_[i * many_children + q, half * rows : (half + 1) * rows, :] = lo
        return 0

    def phases_on(c):
        for j in range(1, nd):
            zp_copy(c, j).wait_recv()
        for j in range(1, nb):
            pf_copy(c, j).start()
        pf[c, b] = zp[c]

    def shifts(c):
        for j in range(1, nb):
            pf_copy(c, j).wait_recv()

        def body(i, _):
            for d in range(nd):
                for j in range(own_tiles):
                    v = pf[c, i, d, j]
                    y = v * v
                    co, si = horner(y, COS), v * horner(y, SIN)
                    for p in range(2):
                        row = d * PER + 2 * (i * own_tiles + j) + p
                        flat[0, pl.ds(row, OCT, stride=R), :] = co
                        flat[1, pl.ds(row, OCT, stride=R), :] = si
            return 0

        lax.fori_loop(0, nb, body, 0)

        def place(o, _):
            rows = pl.ds(pl.multiple_of(o * R, 8), R)
            cc[c, o] = flat[0, rows, :]
            cs[c, o] = flat[1, rows, :]
            return 0

        lax.fori_loop(0, OCT, place, 0)

    def turn(c, o):
        return cc[c, o], cs[c, o]

    tf, tc = thetat_ref.shape
    tl = tc // nd

    def axis(shape, d):
        return lax.broadcasted_iota(I32, shape, d)

    def ones(shape, hit):
        return jnp.where(hit, 1.0, 0.0).astype(BF16)

    def fine_row(i):
        return (i >> 1) & (tf - 1)

    def polar_row(c, r):
        c, r = c + (r >> (R.bit_length() - 1)), r & (R - 1)
        return (r >> (PER.bit_length() - 1)) * tl + c * ROWS + ((r >> 2) & (ROWS - 1))

    def masks():
        shape = (PAIR * R, 4 * tf)
        r, k = axis(shape, 0), axis(shape, 1)
        hit = (((r >> 1) & 1) == jnp.where(k >= 2 * tf, 1, 0)) & ((r & 1) == (k & 1))
        mask[...] = ones(shape, hit)
        shape = (4 * tf, R)
        k, r = axis(shape, 0), axis(shape, 1)
        hit = (((r >> 1) & 1) == jnp.where(k >= 2 * tf, 1, 0)) & ((r & 1) == (k & 1))
        maskt[...] = ones(shape, hit)
        shape = (tf, 4 * tf)
        w = ones(shape, fine_row(axis(shape, 1)) == axis(shape, 0))
        shape = (4 * tf, tf)
        wt = ones(shape, fine_row(axis(shape, 0)) == axis(shape, 1))
        for v, out in zip(split(thetat_ref[...].T), (0, 1)):
            wide[out] = d32(v, w).astype(BF16)
        for v, out in zip(split(thetat_ref[...]), (0, 1)):
            widet[out] = d32(wt, v).astype(BF16)

    d32 = functools.partial(jnp.dot, preferred_element_type=F32)

    def spread_map(c):
        shape = (PAIR * R, tc)
        pick = ones(shape, polar_row(c, axis(shape, 0)) == axis(shape, 1))
        for i, out in enumerate((th, tl_)):
            out[...] = d32(pick, wide[i]).astype(BF16) * mask[...]

    def spread_map_back(c):
        shape = (tc, R)
        pick = ones(shape, polar_row(c, axis(shape, 1)) == axis(shape, 0))
        for i, source in enumerate((0, 0, 1)):
            tth[:, i * R : (i + 1) * R] = d32(widet[source], pick).astype(BF16) * maskt[...]

    gathered = set()

    def aggregate(c):
        c = c // PAIR * PAIR
        if c in gathered:
            return
        gathered.add(c)
        for e in range(PAIR):
            shifts(c + e)
        spread_map(c)

        def body(kk, sums):
            k = 2 * kk
            i0, i1 = itab[PERM, k], itab[PERM, k + 1]
            rh = jnp.concatenate([alh[i0], alh[i1]], axis=1)
            rl = jnp.concatenate([all_[i0], all_[i1]], axis=1)
            v = dot3((th[...], tl_[...]), (rh, rl))
            for q in range(2):
                o, keep = itab[OCTS, k + q], itab[KEEP, k + q].astype(F32)
                for e in range(PAIR):
                    w = v[e * R : (e + 1) * R, q * 128 : (q + 1) * 128]
                    for i, m in enumerate(turn(c + e, o)):
                        sums[2 * e + i] = sums[2 * e + i] * keep + m * w
                for e in range(2 * PAIR):
                    sb[k + q, e] = sums[e]
            return sums

        lax.fori_loop(0, n // 2, body, [jnp.zeros((R, 128), F32)] * (2 * PAIR))

        def pick(p, _):
            last, has = itab[LAST, p], itab[HAS, p].astype(F32)
            for e in range(PAIR):
                v, w = (sb[last, 2 * e + i].reshape(nd * GROUP, 8, 128) for i in range(2))
                below, above = neighbours(w)
                v = (v + jnp.where(even_rows(w.shape), -below, above)) * has
                part[c + e, :, :, p] = v.reshape(nd, GROUP, 8, 128)
            return 0

        lax.fori_loop(0, parents, pick, 0)

    def add(c, d, slot):
        def body(k, _):
            part[c, d, k] = part[c, d, k] + ar[c, slot, k]
            return 0

        lax.fori_loop(0, GROUP, body, 0)

    def send_end(c, j):
        @pl.when(z == 0)
        def _():
            right_copy(c, nd - 1 - j).start()

        @pl.when(z == nd - 1)
        def _():
            left_copy(c, j).start()

    def hop(c, t):
        d, k = nd - 1 + z - t, t - (nd - 1 - z)

        @pl.when(jnp.logical_and(z > 0, t >= z))
        def _():
            up_wait(c, d).wait_recv()
            add(c, d, d)
            right_copy(c, d).start()

        @pl.when(jnp.logical_and(z < nd - 1, k >= 0))
        def _():
            up_wait(c, k).wait_recv()
            add(c, k, k)
            left_copy(c, k).start()

    def finish_up(c):
        @pl.when(z > 0)
        def _():
            up_wait(c, z).wait_recv()
            add(c, z, z)

        @pl.when(z < nd - 1)
        def _():
            up_wait(c, nd).wait_recv()
            add(c, z, nd)

        for j in range(1, nb):
            q_copy(c, j).start()
        qa[c, b] = part[c, z, g]

    started = []

    def translate(c):
        if not started:
            started.append(c)
            for j in range(1, GROUP):
                far_copy(j).wait_recv()
            move = pltpu.make_async_copy(farr, fars, sem_fs)
            move.start()
            move.wait()
            for i in range(C):
                trans_copy(i).wait()
        for j in range(1, nb):
            q_copy(c, j).wait_recv()

        def stage(s, _):
            v = qa[c, s]
            below, above = neighbours(v)
            ql[pl.ds(s * parents, parents), 0] = v
            ql[pl.ds(s * parents, parents), 1] = jnp.where(even_rows(v.shape), below, above)
            return 0

        lax.fori_loop(0, nb, stage, 0)
        even = even_rows((8, 128))
        for jg in range(GROUP):

            def body(p, _):
                u = w = None
                for l in range(many):
                    f, kind = fars[jg, p, l], fars[jg, p, 64 + l]
                    a = trans[c, kind]
                    r, i = a * ql[f, 0], a * ql[f, 1]
                    u = r if u is None else u + r
                    w = i if w is None else w + i
                re = u - pltpu.roll(u, 7, 0)
                im = w + pltpu.roll(w, 1, 0)
                ts[c, jg, p] = jnp.where(even, re, im)
                return 0

            lax.fori_loop(0, parents, body, 0)
        for j in range(1, GROUP):
            t_copy(c, j).start()
        ta[c, g] = ts[c, g]

    def coarse_out(c):
        rows = pl.ds(c * PER, PER)
        return pltpu.make_async_copy(coarse_ref.at[:, rows], coarse_hbm.at[:, rows], sem_c.at[c])

    def coarse(c):
        for j in range(1, GROUP):
            t_copy(c, j).wait_recv()

        def body(p, _):
            rows = pl.ds(c * GROUP * 8, GROUP * 8)
            v = ta[c, :, p] + upper_ref[p, rows, :].reshape(GROUP, 8, 128)
            coarse_ref[p, rows, :] = v.reshape(GROUP * 8, 128)
            cg[c, z, :, p] = v
            return 0

        lax.fori_loop(0, parents, body, 0)
        coarse_out(c).start()

        @pl.when(z < nd - 1)
        def _():
            down_right(c, z).start()

        @pl.when(z > 0)
        def _():
            down_left(c, z).start()

    def pass_down(c, k):
        @pl.when(jnp.logical_and(z >= k, z < nd - 1))
        def _():
            down_right(c, z - k).wait_recv()
            down_right(c, z - k).start()

        @pl.when(jnp.logical_and(z + k < nd, z > 0))
        def _():
            down_left(c, z + k).wait_recv()
            down_left(c, z + k).start()

    spread = []

    def disaggregate(c):
        @pl.when(z == 0)
        def _():
            for d in range(1, nd):
                down_left(c, d).wait_recv()

        @pl.when(z == nd - 1)
        def _():
            for d in range(nd - 1):
                down_right(c, d).wait_recv()

        spread_map_back(c)

        def stage(p, _):
            v = cg[c, :, :, p].reshape(nd * GROUP, 8, 128)
            below, above = neighbours(v)
            xl[p] = v.reshape(R, 128)
            kl[p] = jnp.where(even_rows(v.shape), below, -above).reshape(R, 128)
            return 0

        lax.fori_loop(0, parents, stage, 0)
        spread.append(c)
        first, last = len(spread) == 1, len(spread) == C
        phi = split(phi_ref[...]) if last else None

        def pair(i):
            ys = []
            for q in range(2):
                p, o = itab[PARENT, i + q], itab[OCTANT, i + q]
                co, si = turn(c, o)
                ys.append(co * xl[p] + si * kl[p])
            hi, lo = split(jnp.concatenate(ys, axis=1))
            return d32(tth[...], jnp.concatenate([hi, lo, hi], axis=0))

        def body(ii, _):
            pairs = [pair(4 * ii), pair(4 * ii + 2)]
            for q in range(4):
                i = 4 * ii + q
                w = pairs[q // 2][:, q % 2 * 128 : (q % 2 + 1) * 128]
                if not first:
                    w = w + fa[i]
                if not last:
                    fa[i] = w
                else:
                    half = w.shape[0] // 2
                    line = jnp.concatenate([w[:half], w[half:]], axis=1)
                    fine_ref[i] = dot3(split(line), phi, turned=True)
            if last:
                done = pl.ds(4 * ii, 4)
                pltpu.make_async_copy(fine_ref.at[done], fine_hbm.at[done], sem_f).start()
            return 0

        lax.fori_loop(0, n // 4, body, 0)

    masks()
    for c in use[:PAIR]:
        phases_on(c)
    x_in.wait()
    lax.fori_loop(0, n // many_children, along, 0)
    for c in use[PAIR:]:
        phases_on(c)
    to_scalars.wait()
    upper_in.wait()

    def steps(c):
        yield functools.partial(aggregate, c)
        for j in range(nd - 1):
            yield functools.partial(send_end, c, j)
        for t in range(1, nd - 1):
            yield functools.partial(hop, c, t)
        yield functools.partial(finish_up, c)
        yield functools.partial(translate, c)
        yield functools.partial(coarse, c)
        for k in range(1, nd - 1):
            yield functools.partial(pass_down, c, k)
        yield functools.partial(disaggregate, c)

    each = [list(steps(c)) for c in range(C)]
    for c in order:
        each[c].pop(0)()
    assert not any(each)

    pltpu.make_async_copy(fine_ref, fine_hbm, sem_f).wait()
    for c in range(C):
        coarse_out(c).wait()

    for j in range(1, GROUP):
        far_copy(j).wait_send()

    def drain(c, _):
        for j in range(1, nd):
            zp_copy(c, j).wait_send()
        for j in range(1, nb):
            pf_copy(c, j).wait_send()
            q_copy(c, j).wait_send()
        for j in range(1, GROUP):
            t_copy(c, j).wait_send()
        for d in range(nd):

            @pl.when(d > z)
            def _():
                right_copy(c, d).wait_send()

            @pl.when(d < z)
            def _():
                left_copy(c, d).wait_send()

            @pl.when(jnp.logical_and(d <= z, z < nd - 1))
            def _():
                down_right(c, d).wait_send()

            @pl.when(jnp.logical_and(d >= z, z > 0))
            def _():
                down_left(c, d).wait_send()

        return 0

    lax.fori_loop(0, C, drain, 0)


def shards(
    fine_out,
    theta_interp,
    phi_interp,
    shift_phase,
    translation,
    upper_in,
    children,
    far_boxes,
    far_offsets,
):
    n = fine_out.shape[0]
    tc, tf = theta_interp.shape
    pf_, pc = phi_interp.shape
    parents, many = far_boxes.shape
    nb, nd = lax.axis_size("box"), lax.axis_size("dir")
    noff = translation.shape[0]
    tl = tc // nd
    ROWS = nb // FINE
    GROUP = ROWS // 2
    C = tl // ROWS
    R = nd * GROUP * 8
    PAIR = pair_of(R, C)

    phases = shift_phase.reshape(OCT, tl * 2, 128).transpose(1, 0, 2)

    vmem, smem, hbm = (
        pl.BlockSpec(memory_space=m) for m in (pltpu.VMEM, pltpu.SMEM, pl.ANY)
    )
    dma = pltpu.SemaphoreType.DMA
    tile = (GROUP, parents, 8, 128)
    rows, fine_rows = C * GROUP * 8, tf * 2
    coarse_in, fine_in = pl.pallas_call(
        functools.partial(kernel, (nb, nd, C, ROWS, n, parents, many)),
        in_specs=[smem] + [vmem] * 3 + [hbm] + [vmem] * 2 + [hbm] * 2,
        out_specs=[hbm, hbm],
        out_shape=[
            jax.ShapeDtypeStruct((parents, rows, 128), F32),
            jax.ShapeDtypeStruct((n, fine_rows, pf_), F32),
        ],
        scratch_shapes=[
            pltpu.VMEM((parents, rows, 128), F32),
            pltpu.VMEM((n, fine_rows, pf_), F32),
            pltpu.VMEM((n, fine_rows, pf_), F32),
            pltpu.VMEM((parents, rows, 128), F32),
            pltpu.VMEM((C, noff, 8, 128), F32),
            pltpu.VMEM((8, 128), I32),
            pltpu.SMEM((8, 128), I32),
            pltpu.VMEM((GROUP, parents, 128), I32),
            pltpu.SMEM((GROUP, parents, 128), I32),
            pltpu.VMEM((C, nd, 2 * ROWS // nb, OCT, 128), F32),
            pltpu.VMEM((C, nb, nd, 2 * ROWS // nb, OCT, 128), F32),
            pltpu.VMEM((C, OCT, R, 128), F32),
            pltpu.VMEM((C, OCT, R, 128), F32),
            pltpu.VMEM((2, OCT * R, 128), F32),
            pltpu.VMEM((n, 2 * fine_rows, 128), BF16),
            pltpu.VMEM((n, 2 * fine_rows, 128), BF16),
            pltpu.VMEM((PAIR * R, 4 * tf), BF16),
            pltpu.VMEM((PAIR * R, 4 * tf), BF16),
            pltpu.VMEM((4 * tf, 3 * R), BF16),
            pltpu.VMEM((2, tc, 4 * tf), BF16),
            pltpu.VMEM((2, 4 * tf, tc), BF16),
            pltpu.VMEM((PAIR * R, 4 * tf), BF16),
            pltpu.VMEM((4 * tf, R), BF16),
            pltpu.VMEM((n, 2 * PAIR, R, 128), F32),
            pltpu.VMEM((C, nd) + tile, F32),
            pltpu.VMEM((C, nd + 1) + tile, F32),
            pltpu.VMEM((C, nb) + tile[1:], F32),
            pltpu.VMEM((nb * parents, 2, 8, 128), F32),
            pltpu.VMEM((C,) + tile, F32),
            pltpu.VMEM((C,) + tile, F32),
            pltpu.VMEM((C, nd) + tile, F32),
            pltpu.VMEM((parents, R, 128), F32),
            pltpu.VMEM((parents, R, 128), F32),
            pltpu.VMEM((n, 4 * tf, 128), F32),
            dma,
            dma,
            dma((C,)),
            dma,
            dma((C,)),
            dma,
            dma,
            dma((GROUP,)),
            dma((GROUP,)),
            dma((C, nd)),
            dma((C, nd)),
            dma((C, nb)),
            dma((C, nb)),
            dma((C, nd)),
            dma((C, nd + 1)),
            dma((C, nb)),
            dma((C, nb)),
            dma((C, GROUP)),
            dma((C, GROUP)),
            dma((C, nd)),
            dma((C, nd)),
            dma((C, nd)),
        ],
        compiler_params=pltpu.CompilerParams(
            collective_id=0, has_side_effects=True, vmem_limit_bytes=VMEM_BYTES
        ),
    )(
        children.T,
        far_boxes,
        far_offsets,
        phases,
        rows_view(fine_out),
        phi_interp,
        theta_interp.T,
        rows_view(upper_in),
        rows_view(translation),
    )
    return rows_unview(coarse_in), rows_unview(fine_in)


def solution(mesh):
    placed = (
        P(("box", "dir"), None, None),
        P(),
        P(),
        P(None, "dir"),
        P(None, None, "dir"),
        P("box", None, "dir"),
        P("box", None),
        P("box", None),
        P("box", None),
    )
    return jax.shard_map(
        shards,
        mesh=mesh,
        in_specs=placed,
        out_specs=(P("box", None, "dir"), P(("box", "dir"), None, None)),
        check_vma=False,
    )
```
